256 devices in a mesh: pair: 64 (over y_hi, x, z), virt: 4 (over y_lo, core).
Axes of the slice: x: 4, y: 4 (y_hi: 2, y_lo: 2; y = y_hi * 2 + y_lo), z: 8, core: 2. Of those that a mesh axis runs over, the one named last changes fastest.
Arguments:
- t2_amps: bfloat16 [4, 64, 1600, 1600], P(None, 'pair', None, 'virt'), may hold values from -2 to 2
- l2_amps: bfloat16 [4, 64, 1600, 1600], P(None, 'pair', None, 'virt'), may hold values from -2 to 2
- panel_start: int32 [2], replicated, may hold values from 0 to 368
Outputs:
- dens_vvvv: bfloat16 [2, 128, 128, 128, 128], P(None, None, 'virt', 'pair')
- dens_ovov: bfloat16 [2, 128, 4, 4, 128], P(None, 'pair', None, None, 'virt')
The draws below stay inside these ranges and needn't reach their ends.
Inputs may be any that keep to these rules, and one draw needn't show every extreme that they name: `panel_start`: offsets inside a virtual block.
All inputs are finite; a program needn't handle non-finite values.
Results may differ from the reference program's by a relative error of at most 0.0018.
Values may be sent and summed in bfloat16 or wider, within the bound.
No kernel may reach another device: no remote copies, remote signals or barrier semaphores. Data moves between devices by JAX's collectives and lax.ppermute only.
A program may use at most 128 MiB of HBM per device.

```python
import jax
import jax.numpy as jnp

VIRTUALS = 1600
OCC_I = 4
PANEL = 128
OCC_K = 64
N_VIRT = 4


def shard_levels(key, dims, shards, low, top_value):
    factor_of = 1.0
    for dim, parts in shards:
        heights = jax.random.uniform(jax.random.fold_in(jax.random.fold_in(key, 6), dim), (parts,), jnp.float32, low / len(shards), top_value / len(shards))
        factor_of = factor_of * jnp.repeat(jnp.exp(heights), dims[dim] // parts).reshape((-1,) + (1,) * (len(dims) - 1 - dim))
    return factor_of


def centred(stream_key, shape, deviation, most, shards=(), held_as=jnp.bfloat16):
    gain = shard_levels(stream_key, shape, shards, -0.22, 0.18) if shards else 1.0
    result = jax.random.normal(stream_key, shape, jnp.float32) * deviation * gain
    return jnp.minimum(jnp.maximum(result, -most), most).astype(held_as)


def setup_inputs(seed: int = 0) -> dict:
    splits = jax.random.split(jax.random.key(seed), 4)
    t2_amps = centred(splits[0], (OCC_I, OCC_K, VIRTUALS, VIRTUALS), 0.3, 2.0, ((1, 64), (3, 4)))
    l2_amps = centred(splits[1], (OCC_I, OCC_K, VIRTUALS, VIRTUALS), 0.3, 2.0, ((1, 64), (3, 4)))
    panel_start = jax.random.randint(splits[2], (2,), 0, VIRTUALS // N_VIRT - PANEL // N_VIRT + 1).astype(jnp.int32)
    return {"t2_amps": t2_amps, "l2_amps": l2_amps, "panel_start": panel_start}


def panel_index(start):
    width = VIRTUALS // N_VIRT
    piece = PANEL // N_VIRT
    index = jnp.arange(N_VIRT, dtype=jnp.int32)[:, None] * width + start + jnp.arange(piece, dtype=jnp.int32)[None, :]
    return index.reshape(-1).astype(jnp.int32)


def cut_panel(amps, index):
    rows = jnp.take(amps, index, axis=2)
    return jnp.take(rows, index, axis=3)


def reference(t2_amps, l2_amps, panel_start):
    vvvv_list = []
    ovov_list = []
    for panel in range(2):
        index = panel_index(panel_start[panel])
        amp_panel = cut_panel(t2_amps, index)
        lam_panel = cut_panel(l2_amps, index)
        pairs = OCC_I * OCC_K
        left = amp_panel.reshape(pairs, PANEL * PANEL)
        right = lam_panel.reshape(pairs, PANEL * PANEL)
        block = jnp.dot(left.T, right, preferred_element_type=jnp.float32)
        vvvv_list.append((0.5 * block).astype(jnp.bfloat16).reshape(PANEL, PANEL, PANEL, PANEL))
        cycle = jnp.einsum("jkbc,ikac->bjia", amp_panel.astype(jnp.float32), lam_panel.astype(jnp.float32))
        ovov_list.append((-cycle).astype(jnp.bfloat16))
    return jnp.stack(vvvv_list), jnp.stack(ovov_list)
```

```python
import jax
import jax.numpy as jnp
from jax import lax
from jax.sharding import PartitionSpec as P

NZ = 8
NXY = 8
PAIRS = NZ * NXY
PANELS = 2
NV = 4
Z_GROUPS = [[xy * NZ + z for z in range(NZ)] for xy in range(NXY)]
XY_GROUPS = [[xy * NZ + z for xy in range(NXY)] for z in range(NZ)]


def cut(amps, start, piece):
    rows = lax.dynamic_slice_in_dim(amps, start, piece, 1)
    occ, _, virtuals = rows.shape
    rows = rows.reshape(occ, piece, NV, virtuals // NV)
    return lax.dynamic_slice_in_dim(rows, start, piece, 3).reshape(occ, piece, NV * piece)


def spread(block, groups):
    many = jnp.broadcast_to(block[None], (len(groups[0]),) + block.shape)
    return lax.all_to_all(many, "pair", 0, 0, axis_index_groups=groups)


def shards(t2_amps, l2_amps, panel_start):
    piece = 128 // NV
    amps = jnp.transpose(t2_amps[:, 0], (0, 2, 1))
    lams = jnp.transpose(l2_amps[:, 0], (0, 2, 1))
    tp = jnp.stack([cut(amps, panel_start[p], piece) for p in range(PANELS)])
    lp = jnp.stack([cut(lams, panel_start[p], piece) for p in range(PANELS)])
    occ = tp.shape[1]
    own = lp.reshape(PANELS, occ, piece, PAIRS, 2).transpose(3, 0, 1, 4, 2)
    own = lax.all_to_all(own.reshape(PAIRS, 4, 128), "pair", 0, 0)
    own = own.reshape(PAIRS, PANELS, occ, 2, piece)
    wide = lax.all_gather(own.reshape(PAIRS * 4, 128), "virt").reshape(NV, PAIRS, PANELS, occ, 2, piece)
    wide = wide.transpose(1, 2, 3, 4, 0, 5).reshape(PAIRS, PANELS, occ, 2, NV * piece)
    near = spread(tp.reshape(-1, 128), Z_GROUPS)
    far = spread(near.reshape(-1, 128), XY_GROUPS)
    far = far.reshape(PAIRS, PANELS, occ, piece, NV * piece)
    part = -jnp.einsum("kpjcb,kpiac->pbjia", far, own, preferred_element_type=jnp.float32)
    part = part.reshape(PANELS, PAIRS, 2, occ, occ, 2).transpose(1, 0, 2, 3, 4, 5)
    part = lax.all_to_all(part.reshape(PAIRS, 1, 128), "pair", 0, 0)
    part = part.reshape(NV, PAIRS // NV, PANELS, 2, occ, occ, 2)
    part = lax.all_to_all(part.reshape(NV, 16, 128), "virt", 0, 0)
    part = part.reshape(NV, PAIRS // NV, PANELS, 2, occ, occ, 2)
    ovov = part.sum(0).transpose(1, 2, 3, 4, 0, 5).reshape(PANELS, 2, occ, occ, piece).astype(jnp.bfloat16)
    vvvv = 0.5 * jnp.einsum("kpiba,kpicd->pabcd", far, wide, preferred_element_type=jnp.float32)
    return vvvv.astype(jnp.bfloat16), ovov


def solution(mesh):
    in_specs = (P(None, "pair", None, "virt"), P(None, "pair", None, "virt"), P())
    out_specs = (P(None, None, "virt", "pair", None), P(None, "pair", None, None, "virt"))
    return jax.shard_map(shards, mesh=mesh, in_specs=in_specs, out_specs=out_specs, check_vma=False)
```

```python
import functools

import jax
import jax.numpy as jnp
from jax import lax
from jax.experimental import pallas as pl
from jax.experimental.pallas import tpu as pltpu
from jax.sharding import PartitionSpec as P

NZ = 8
NX = 4
NY = 2
NXY = NX * NY
PAIRS = NZ * NXY
PANELS = 2
NV = 4
OCC = 4
PANEL = 128
PIECE = PANEL // NV
LANES = 128
VIRTUALS = 1600
WIDTH = VIRTUALS // NV
WINDOW = PIECE + 16
HEAD = VIRTUALS // LANES * LANES
AMP_ROWS = PANELS * OCC * PIECE
LAM_ROWS = PANELS * 16
Z_GROUPS = [[xy * NZ + z for z in range(NZ)] for xy in range(NXY)]
X_SHIFTS = (1, 3, 2)
HALF = AMP_ROWS // PANELS
PART_ROWS = 64
OWN_ROWS = NZ * PANELS * 2


def pair_shift(dy, dx):
    return [
        ((y * NX + x) * NZ + z, (((y + dy) % NY) * NX + (x + dx) % NX) * NZ + z)
        for y in range(NY)
        for x in range(NX)
        for z in range(NZ)
    ]


def cut_kernel(start_ref, amp_ref, lam_ref, out_ref, buf, rows, sems):
    copies = []
    for a, src in enumerate((amp_ref, lam_ref)):
        for p in range(PANELS):
            base = jnp.minimum(start_ref[p] // 16 * 16, WIDTH - WINDOW)
            base = pl.multiple_of(base, 16)
            copy = pltpu.make_async_copy(
                src.at[:, pl.ds(base, WINDOW), :], buf.at[a, p], sems.at[a, p]
            )
            copy.start()
            copies.append((a, p, copy))
    lane = lax.broadcasted_iota(jnp.int32, (1, LANES), 1)
    place = (4 * (lane % 32) + lane // 32, 16 * ((lane % 16) // 2) + 2 * (lane // 16) + lane % 2)
    virt = lax.broadcasted_iota(jnp.int32, (HEAD + LANES, LANES), 0)
    for a, p, copy in copies:
        start = start_ref[p]
        offset = start - jnp.minimum(start // 16 * 16, WIDTH - WINDOW)
        target = place[a] // PIECE * WIDTH + start + place[a] % PIECE
        pick = jnp.where(virt == target, 1.0, 0.0).astype(jnp.bfloat16)
        copy.wait()
        head = buf[a, p, :, :, :HEAD].reshape(OCC * WINDOW, HEAD)
        tail = buf[a, p, :, :, HEAD:].reshape(OCC * WINDOW, VIRTUALS - HEAD)
        blank = jnp.zeros((OCC * WINDOW, HEAD + LANES - VIRTUALS), jnp.bfloat16)
        tail = jnp.concatenate([tail, blank], axis=1)
        rows[...] = jnp.dot(head, pick[:HEAD], preferred_element_type=jnp.float32) + jnp.dot(
            tail, pick[HEAD:], preferred_element_type=jnp.float32
        )
        mine = jnp.concatenate([rows[pl.ds(i * WINDOW + offset, PIECE), :] for i in range(OCC)], axis=0)
        turned = mine.T
        if a == 0:
            for i in range(OCC):
                cells = [
                    turned[PIECE * q : PIECE * (q + 1), PIECE * i : PIECE * (i + 1)] for q in range(4)
                ]
                block = jnp.concatenate(cells, axis=1).astype(jnp.bfloat16)
                for z in range(NZ):
                    out_ref[z, pl.ds((p * OCC + i) * PIECE, PIECE), :] = block
        else:
            block = turned.astype(jnp.bfloat16)
            for z in range(NZ):
                out_ref[z, pl.ds(AMP_ROWS + 16 * p, 16), :] = block[16 * z : 16 * (z + 1)]


def cut(panel_start, amps, lams):
    return pl.pallas_call(
        cut_kernel,
        out_shape=jax.ShapeDtypeStruct((NZ, AMP_ROWS + LAM_ROWS, LANES), jnp.bfloat16),
        in_specs=[
            pl.BlockSpec(memory_space=pltpu.SMEM),
            pl.BlockSpec(memory_space=pltpu.HBM),
            pl.BlockSpec(memory_space=pltpu.HBM),
        ],
        out_specs=pl.BlockSpec(memory_space=pltpu.VMEM),
        scratch_shapes=[
            pltpu.VMEM((2, PANELS, OCC, WINDOW, VIRTUALS), jnp.bfloat16),
            pltpu.VMEM((OCC * WINDOW, LANES), jnp.float32),
            pltpu.SemaphoreType.DMA((2, PANELS)),
        ],
        compiler_params=pltpu.CompilerParams(vmem_limit_bytes=60 * 2**20),
        name="cut_panels",
    )(panel_start, amps, lams)


def line_kernel(place_ref, near_ref, rows_ref, here_ref, there_ref, wide, pick, prod, own):
    y, x = place_ref[0], place_ref[1]
    for p in range(PANELS):
        for k in range(NZ):
            part = near_ref[k, pl.ds(p * HALF, HALF), :]
            wide[pl.ds(k * HALF, HALF), :] = part.astype(jnp.float32)
        for r in range(PIECE):
            rows_ref[p, :, pl.ds(r * LANES, LANES)] = wide[pl.ds(r, NZ * OCC, PIECE), :].astype(jnp.bfloat16)
    lane = lax.broadcasted_iota(jnp.int32, (16, LANES), 1) // PIECE
    for p in range(PANELS):
        for k in range(NZ):
            lam = near_ref[k, pl.ds(AMP_ROWS + 16 * p, 16), :].astype(jnp.float32)
            own[k, p] = lam
            for d in range(4):
                turned = lam if d == 0 else pltpu.roll(lam, PIECE * d, 1)
                for q in range(4):
                    i = (q - d) % 4
                    cell = jnp.where(lane == q, turned, 0.0)
                    for v in range(NV):
                        row = q // 2 * LANES + v * PIECE + q % 2 * 16 + i * 4
                        pick[pl.ds(row, 4), pl.ds(k * LANES, LANES)] = cell[4 * v : 4 * v + 4]
        amp = jnp.concatenate([near_ref[k, pl.ds(p * HALF, HALF), :] for k in range(NZ)], axis=1)
        full = lax.dot_general(
            amp, pick[...].astype(jnp.bfloat16), (((1,), (1,)), ((), ())), preferred_element_type=jnp.float32
        )
        prod[p, 0] = full[:, :LANES]
        prod[p, 1] = full[:, LANES:]
    for dy, ref in enumerate((here_ref, there_ref)):
        for dx in range(NX):
            xy = lax.rem(y + dy, NY) * NX + lax.rem(x + dx, NX)
            for p in range(PANELS):
                for r in range(4):
                    for qh in range(2):
                        cell = prod[p, qh, pl.ds(4 * xy + r, OCC, PIECE), :]
                        ref[dx, pl.ds((2 * r + qh) * 8 + 4 * p, OCC), :] = cell
                for k in range(NZ):
                    ref[dx, pl.ds(PART_ROWS + k * 4 + p * 2, 2), :] = own[k, p, pl.ds(2 * xy, 2), :]


def line_share(place, near):
    sent = jax.ShapeDtypeStruct((NX, PART_ROWS + OWN_ROWS, LANES), jnp.float32)
    vmem = pl.BlockSpec(memory_space=pltpu.VMEM)
    return pl.pallas_call(
        line_kernel,
        out_shape=(jax.ShapeDtypeStruct((PANELS, NZ * OCC, PIECE * LANES), jnp.bfloat16), sent, sent),
        in_specs=[pl.BlockSpec(memory_space=pltpu.SMEM), vmem],
        out_specs=(vmem, vmem, vmem),
        scratch_shapes=[
            pltpu.VMEM((NZ * HALF, LANES), jnp.float32),
            pltpu.VMEM((2 * LANES, NZ * LANES), jnp.float32),
            pltpu.VMEM((PANELS, 2, HALF, LANES), jnp.float32),
            pltpu.VMEM((NZ, PANELS, 16, LANES), jnp.float32),
        ],
        compiler_params=pltpu.CompilerParams(vmem_limit_bytes=24 * 2**20),
        name="line_share",
    )(place, near)


def merge_kernel(*refs):
    ins, out_ref = refs[:NX], refs[NX]
    total = ins[0][pl.ds(0, PART_ROWS), :]
    for ref in ins[1:]:
        total = total + ref[pl.ds(0, PART_ROWS), :]
    for n, ref in enumerate(ins):
        rows = ref[pl.ds(PART_ROWS, 2 * OWN_ROWS), :]
        out_ref[pl.ds(n * 2 * OWN_ROWS, 2 * OWN_ROWS), :] = rows.astype(jnp.bfloat16)
    high = total.astype(jnp.bfloat16)
    out_ref[pl.ds(NXY * OWN_ROWS, PART_ROWS), :] = high
    out_ref[pl.ds(NXY * OWN_ROWS + PART_ROWS, PART_ROWS), :] = (total - high.astype(jnp.float32)).astype(jnp.bfloat16)


def merge(got):
    vmem = pl.BlockSpec(memory_space=pltpu.VMEM)
    return pl.pallas_call(
        merge_kernel,
        out_shape=jax.ShapeDtypeStruct((NXY * OWN_ROWS + 2 * PART_ROWS, LANES), jnp.bfloat16),
        in_specs=[vmem] * NX,
        out_specs=vmem,
        compiler_params=pltpu.CompilerParams(vmem_limit_bytes=8 * 2**20),
        name="merge_shares",
    )(*got)


def lam_kernel(own_ref, line_ref, part_ref, wide, rows):
    lane = lax.broadcasted_iota(jnp.int32, (NXY * NZ, LANES), 1) // PIECE
    count = NXY * OWN_ROWS
    wide[...] = own_ref[:, pl.ds(0, count), :].astype(jnp.float32)
    for p in range(PANELS):
        for g in range(2):
            parts = [wide[v, pl.ds(2 * p + g, NXY * NZ, 4), :] for v in range(NV)]
            for i in range(OCC):
                cell = jnp.zeros((NXY * NZ, LANES), jnp.float32)
                for v in range(NV):
                    turn = PIECE * ((v - i) % 4)
                    part = parts[v] if turn == 0 else pltpu.roll(parts[v], turn, 1)
                    cell = jnp.where(lane == v, part, cell)
                rows[pl.ds(i, NXY * NZ, OCC), :] = cell
            line_ref[p, :, pl.ds(g * LANES, LANES)] = rows[...].astype(jnp.bfloat16)
    total = jnp.zeros((PART_ROWS, LANES), jnp.float32)
    for v in range(NV):
        for n in range(2):
            total = total + own_ref[v, pl.ds(count + n * PART_ROWS, PART_ROWS), :].astype(jnp.float32)
    part_ref[...] = total.reshape(NZ, PART_ROWS // NZ, LANES)


def lam_matrix(own):
    vmem = pl.BlockSpec(memory_space=pltpu.VMEM)
    matrix = jax.ShapeDtypeStruct((PANELS, PAIRS * OCC, 2 * LANES), jnp.bfloat16)
    return pl.pallas_call(
        lam_kernel,
        out_shape=(matrix, jax.ShapeDtypeStruct((NZ, PART_ROWS // NZ, LANES), jnp.float32)),
        in_specs=[vmem],
        out_specs=(vmem, vmem),
        scratch_shapes=[
            pltpu.VMEM((NV, NXY * OWN_ROWS, LANES), jnp.float32),
            pltpu.VMEM((PAIRS * OCC, LANES), jnp.float32),
        ],
        compiler_params=pltpu.CompilerParams(vmem_limit_bytes=16 * 2**20),
        name="lam_matrix",
    )(own)


STEP = 8


def vvvv_kernel(*refs):
    blocks, lam_ref, out_ref, wide = refs[:NXY], refs[NXY], refs[NXY + 1], refs[NXY + 2]
    amp = jnp.concatenate([b[0] for b in blocks], axis=0)
    prod = lax.dot_general(amp, lam_ref[0], (((0,), (0,)), ((), ())), preferred_element_type=jnp.float32)
    prod = prod * 0.5
    wide[pl.ds(0, STEP * LANES, 2), :] = prod[:, :LANES]
    wide[pl.ds(1, STEP * LANES, 2), :] = prod[:, LANES:]
    out_ref[...] = wide[...].astype(jnp.bfloat16)


def vvvv_product(blocks, lam):
    steps = PIECE // STEP
    block_spec = pl.BlockSpec((1, NZ * OCC, STEP * LANES), lambda p, r: (p, 0, r))
    out = pl.pallas_call(
        vvvv_kernel,
        out_shape=jax.ShapeDtypeStruct((PANELS * PANEL * PIECE * 2, LANES), jnp.bfloat16),
        grid=(PANELS, steps),
        in_specs=[block_spec] * NXY + [pl.BlockSpec((1, PAIRS * OCC, 2 * LANES), lambda p, r: (p, 0, 0))],
        out_specs=pl.BlockSpec((STEP * 2 * LANES, LANES), lambda p, r: (p * steps + r, 0)),
        scratch_shapes=[pltpu.VMEM((STEP * 2 * LANES, LANES), jnp.float32)],
        compiler_params=pltpu.CompilerParams(vmem_limit_bytes=32 * 2**20),
        name="vvvv_product",
    )(*blocks, lam)
    return out.reshape(PANELS, PANEL, PIECE, 2, LANES)


def send(block, dy, dx):
    return lax.ppermute(block, "pair", pair_shift(dy, dx))


def after(value, *others):
    return lax.optimization_barrier((value,) + others)[0]


def shards(t2_amps, l2_amps, panel_start):
    amps = jnp.transpose(t2_amps[:, 0], (0, 2, 1))
    lams = jnp.transpose(l2_amps[:, 0], (0, 2, 1))
    xy = lax.axis_index("pair") // NZ
    place = jnp.stack([xy // NX, xy % NX]).astype(jnp.int32)
    near = lax.all_to_all(cut(panel_start, amps, lams), "pair", 0, 0, axis_index_groups=Z_GROUPS)
    held, here, there = line_share(place, near)

    other = send(held, 1, 0)
    beside = {dx: send(held, 0, dx) for dx in X_SHIFTS}

    there = send(there, 1, 0)
    part = here[:, :PART_ROWS] + there[:, :PART_ROWS]
    pay = jnp.concatenate([part, here[:, PART_ROWS:], there[:, PART_ROWS:]], axis=1)
    pay = after(pay, other)
    own = merge([pay[0]] + [send(pay[dx], 0, dx) for dx in X_SHIFTS])
    own = after(own, *beside.values())
    lam, part = lam_matrix(lax.all_gather(own, "virt"))

    cross = {1: send(other, 0, 1), 3: send(other, 0, 3), 2: send(beside[2], 1, 0)}
    blocks = [held, other]
    for dx in X_SHIFTS:
        blocks += [beside[dx], cross[dx]]

    part = after(part, *cross.values())
    part = lax.all_to_all(part, "pair", 0, 0, axis_index_groups=Z_GROUPS)
    part = lax.dynamic_slice_in_dim(part, lax.axis_index("virt") * PIECE, PIECE, 2)
    part = part.reshape(NZ, PANELS, OCC, 2, OCC, 2, 2).transpose(1, 3, 2, 4, 5, 0, 6)
    ovov = (-part).reshape(PANELS, 2, OCC, OCC, PIECE).astype(jnp.bfloat16)
    return vvvv_product(blocks, lam), ovov


def solution(mesh):
    in_specs = (P(None, "pair", None, "virt"), P(None, "pair", None, "virt"), P())
    out_specs = (P(None, None, "virt", "pair", None), P(None, "pair", None, None, "virt"))
    return jax.shard_map(shards, mesh=mesh, in_specs=in_specs, out_specs=out_specs, check_vma=False)
```

```python
import functools

import jax
import jax.numpy as jnp
from jax import lax
from jax.experimental import pallas as pl
from jax.experimental.pallas import tpu as pltpu
from jax.sharding import PartitionSpec as P

NZ = 8
NX = 4
NY = 2
NXY = NX * NY
PAIRS = NZ * NXY
PANELS = 2
NV = 4
OCC = 4
PANEL = 128
PIECE = PANEL // NV
LANES = 128
VIRTUALS = 1600
WIDTH = VIRTUALS // NV
WINDOW = PIECE + 16
HEAD = VIRTUALS // LANES * LANES
AMP_ROWS = PANELS * OCC * PIECE
LAM_ROWS = PANELS * PANEL
Z_GROUPS = [[xy * NZ + z for z in range(NZ)] for xy in range(NXY)]
X_SHIFTS = (1, 3, 2)
HALF = AMP_ROWS // PANELS
PART_ROWS = 64
OWN_ROWS = NXY * PANELS * 2


def pair_shift(dy, dx):
    return [
        ((y * NX + x) * NZ + z, (((y + dy) % NY) * NX + (x + dx) % NX) * NZ + z)
        for y in range(NY)
        for x in range(NX)
        for z in range(NZ)
    ]


def cut_kernel(start_ref, amp_ref, lam_ref, line_ref, own_ref, buf, rows, sems):
    copies = []
    for a, src in enumerate((amp_ref, lam_ref)):
        for p in range(PANELS):
            base = jnp.minimum(start_ref[p] // 16 * 16, WIDTH - WINDOW)
            base = pl.multiple_of(base, 16)
            copy = pltpu.make_async_copy(
                src.at[:, pl.ds(base, WINDOW), :], buf.at[a, p], sems.at[a, p]
            )
            copy.start()
            copies.append((a, p, copy))
    lane = lax.broadcasted_iota(jnp.int32, (1, LANES), 1)
    order = (4 * (lane % 32) + lane // 32, lane)
    virt = lax.broadcasted_iota(jnp.int32, (HEAD + LANES, LANES), 0)
    for a, p, copy in copies:
        start = start_ref[p]
        offset = start - jnp.minimum(start // 16 * 16, WIDTH - WINDOW)
        target = order[a] // PIECE * WIDTH + start + order[a] % PIECE
        pick = jnp.where(virt == target, 1.0, 0.0).astype(jnp.bfloat16)
        copy.wait()
        head = buf[a, p, :, :, :HEAD].reshape(OCC * WINDOW, HEAD)
        tail = buf[a, p, :, :, HEAD:].reshape(OCC * WINDOW, VIRTUALS - HEAD)
        blank = jnp.zeros((OCC * WINDOW, HEAD + LANES - VIRTUALS), jnp.bfloat16)
        tail = jnp.concatenate([tail, blank], axis=1)
        rows[...] = jnp.dot(head, pick[:HEAD], preferred_element_type=jnp.float32) + jnp.dot(
            tail, pick[HEAD:], preferred_element_type=jnp.float32
        )
        mine = jnp.concatenate([rows[pl.ds(i * WINDOW + offset, PIECE), :] for i in range(OCC)], axis=0)
        turned = mine.T
        if a == 0:
            for i in range(OCC):
                cells = [
                    turned[PIECE * q : PIECE * (q + 1), PIECE * i : PIECE * (i + 1)] for q in range(4)
                ]
                block = jnp.concatenate(cells, axis=1).astype(jnp.bfloat16)
                own_ref[pl.ds((p * OCC + i) * PIECE, PIECE), :] = block
                for z in range(NZ):
                    line_ref[z, pl.ds((p * OCC + i) * PIECE, PIECE), :] = block
        else:
            own_ref[pl.ds(AMP_ROWS + p * PANEL, PANEL), :] = turned.astype(jnp.bfloat16)


def cut(panel_start, amps, lams):
    return pl.pallas_call(
        cut_kernel,
        out_shape=(
            jax.ShapeDtypeStruct((NZ, AMP_ROWS, LANES), jnp.bfloat16),
            jax.ShapeDtypeStruct((AMP_ROWS + LAM_ROWS, LANES), jnp.bfloat16),
        ),
        in_specs=[
            pl.BlockSpec(memory_space=pltpu.SMEM),
            pl.BlockSpec(memory_space=pltpu.HBM),
            pl.BlockSpec(memory_space=pltpu.HBM),
        ],
        out_specs=(pl.BlockSpec(memory_space=pltpu.VMEM),) * 2,
        scratch_shapes=[
            pltpu.VMEM((2, PANELS, OCC, WINDOW, VIRTUALS), jnp.bfloat16),
            pltpu.VMEM((OCC * WINDOW, LANES), jnp.float32),
            pltpu.SemaphoreType.DMA((2, PANELS)),
        ],
        compiler_params=pltpu.CompilerParams(vmem_limit_bytes=60 * 2**20),
        name="cut_panels",
    )(panel_start, amps, lams)


def rows_kernel(near_ref, out_ref, wide):
    for p in range(PANELS):
        for k in range(NZ):
            part = near_ref[k, pl.ds(p * HALF, HALF), :]
            wide[pl.ds(k * HALF, HALF), :] = part.astype(jnp.float32)
        for r in range(PIECE):
            out_ref[p, :, pl.ds(r * LANES, LANES)] = wide[pl.ds(r, NZ * OCC, PIECE), :].astype(jnp.bfloat16)


def to_rows(near):
    vmem = pl.BlockSpec(memory_space=pltpu.VMEM)
    return pl.pallas_call(
        rows_kernel,
        out_shape=jax.ShapeDtypeStruct((PANELS, NZ * OCC, PIECE * LANES), jnp.bfloat16),
        in_specs=[vmem],
        out_specs=vmem,
        scratch_shapes=[pltpu.VMEM((NZ * HALF, LANES), jnp.float32)],
        compiler_params=pltpu.CompilerParams(vmem_limit_bytes=16 * 2**20),
        name="occupied_rows",
    )(near)


def plane_kernel(place_ref, *refs):
    ins, out_ref, pick, prod, wide, own = refs[:NXY], *refs[NXY:]
    xy = place_ref[0]
    lane = lax.broadcasted_iota(jnp.int32, (OCC * 4, LANES), 1) // PIECE
    for p in range(PANELS):
        for s in range(NXY):
            wide[...] = ins[s][pl.ds(p * HALF, HALF), :].astype(jnp.float32)
            amp = jnp.concatenate([wide[pl.ds(j * PIECE + 4 * xy, 4), :] for j in range(OCC)], axis=0)
            for d in range(4):
                turned = amp if d == 0 else pltpu.roll(amp, PIECE * d, 1)
                for i in range(OCC):
                    q = (i - d) % 4
                    cell = jnp.where(lane == i, turned, 0.0)
                    for j in range(OCC):
                        row = q * 16 + j * 4 + i
                        pick[s, pl.ds(row, 4, 64), :] = cell[4 * j : 4 * j + 4]
            row = pl.multiple_of(AMP_ROWS + p * PANEL + 16 * xy, 16)
            own[s, p] = ins[s][pl.ds(row, 16), :].astype(jnp.float32)
        amp = jnp.concatenate([pick[s].astype(jnp.bfloat16) for s in range(NXY)], axis=1)
        lam = jnp.concatenate([ins[s][pl.ds(AMP_ROWS + p * PANEL, PANEL), :] for s in range(NXY)], axis=1)
        prod[...] = lax.dot_general(amp, lam, (((1,), (1,)), ((), ())), preferred_element_type=jnp.float32)
        for z in range(NZ):
            out_ref[z, pl.ds(p * 32, 32), :] = prod[pl.ds(z * 32, 32), :]
    for z in range(NZ):
        for s in range(NXY):
            for p in range(PANELS):
                out_ref[z, pl.ds(PART_ROWS + s * 4 + p * 2, 2), :] = own[s, p, pl.ds(2 * z, 2), :]


def plane_share(place, parts):
    vmem = pl.BlockSpec(memory_space=pltpu.VMEM)
    return pl.pallas_call(
        plane_kernel,
        out_shape=jax.ShapeDtypeStruct((NZ, PART_ROWS + OWN_ROWS, LANES), jnp.float32),
        in_specs=[pl.BlockSpec(memory_space=pltpu.SMEM)] + [vmem] * NXY,
        out_specs=vmem,
        scratch_shapes=[
            pltpu.VMEM((NXY, 2 * LANES, LANES), jnp.float32),
            pltpu.VMEM((2 * LANES, LANES), jnp.float32),
            pltpu.VMEM((HALF, LANES), jnp.float32),
            pltpu.VMEM((NXY, PANELS, 16, LANES), jnp.float32),
        ],
        compiler_params=pltpu.CompilerParams(vmem_limit_bytes=16 * 2**20),
        name="plane_share",
    )(place, *parts)


def pack_kernel(in_ref, out_ref, rows):
    total = in_ref[0, pl.ds(0, PART_ROWS), :]
    for z in range(1, NZ):
        total = total + in_ref[z, pl.ds(0, PART_ROWS), :]
    for z in range(NZ):
        for s in range(NXY):
            rows[pl.ds((s * NZ + z) * 4, 4), :] = in_ref[z, pl.ds(PART_ROWS + s * 4, 4), :]
    out_ref[pl.ds(0, NZ * OWN_ROWS), :] = rows[...].astype(jnp.bfloat16)
    high = total.astype(jnp.bfloat16)
    out_ref[pl.ds(NZ * OWN_ROWS, PART_ROWS), :] = high
    out_ref[pl.ds(NZ * OWN_ROWS + PART_ROWS, PART_ROWS), :] = (total - high.astype(jnp.float32)).astype(jnp.bfloat16)


def pack(got):
    vmem = pl.BlockSpec(memory_space=pltpu.VMEM)
    return pl.pallas_call(
        pack_kernel,
        out_shape=jax.ShapeDtypeStruct((NZ * OWN_ROWS + 2 * PART_ROWS, LANES), jnp.bfloat16),
        in_specs=[vmem],
        out_specs=vmem,
        scratch_shapes=[pltpu.VMEM((NZ * OWN_ROWS, LANES), jnp.float32)],
        compiler_params=pltpu.CompilerParams(vmem_limit_bytes=8 * 2**20),
        name="pack_shares",
    )(got)


def lam_kernel(place_ref, own_ref, line_ref, part_ref, wide, rows):
    lane = lax.broadcasted_iota(jnp.int32, (NXY * NZ, LANES), 1) // PIECE
    count = NXY * OWN_ROWS
    wide[...] = own_ref[:, pl.ds(0, count), :].astype(jnp.float32)
    for p in range(PANELS):
        for g in range(2):
            parts = [wide[v, pl.ds(2 * p + g, NXY * NZ, 4), :] for v in range(NV)]
            for i in range(OCC):
                cell = jnp.zeros((NXY * NZ, LANES), jnp.float32)
                for v in range(NV):
                    turn = PIECE * ((v - i) % 4)
                    part = parts[v] if turn == 0 else pltpu.roll(parts[v], turn, 1)
                    cell = jnp.where(lane == v, part, cell)
                rows[pl.ds(i, NXY * NZ, OCC), :] = cell
            line_ref[p, :, pl.ds(g * LANES, LANES)] = rows[...].astype(jnp.bfloat16)
    total = jnp.zeros((PART_ROWS, LANES), jnp.float32)
    for v in range(NV):
        for n in range(2):
            total = total + own_ref[v, pl.ds(count + n * PART_ROWS, PART_ROWS), :].astype(jnp.float32)
    mine = pltpu.roll(-total, lax.rem(LANES - place_ref[1] * PIECE, LANES), 1)
    part_ref[...] = mine[:, :PIECE].astype(jnp.bfloat16)


def lam_matrix(place, own):
    vmem = pl.BlockSpec(memory_space=pltpu.VMEM)
    matrix = jax.ShapeDtypeStruct((PANELS, PAIRS * OCC, 2 * LANES), jnp.bfloat16)
    return pl.pallas_call(
        lam_kernel,
        out_shape=(matrix, jax.ShapeDtypeStruct((PART_ROWS, PIECE), jnp.bfloat16)),
        in_specs=[pl.BlockSpec(memory_space=pltpu.SMEM), vmem],
        out_specs=(vmem, vmem),
        scratch_shapes=[
            pltpu.VMEM((NV, NXY * OWN_ROWS, LANES), jnp.float32),
            pltpu.VMEM((PAIRS * OCC, LANES), jnp.float32),
        ],
        compiler_params=pltpu.CompilerParams(vmem_limit_bytes=16 * 2**20),
        name="lam_matrix",
    )(place, own)


CHUNK = 1024
SLOTS = 4


def vvvv_kernel(*refs):
    blocks, lam_ref, part_ref, out_ref, ovov_ref, wide, stage, sems = refs[:NXY], *refs[NXY:]
    part_copy = pltpu.make_async_copy(part_ref, ovov_ref, sems.at[SLOTS])
    part_copy.start()
    chunks = PANELS * PIECE * LANES // CHUNK

    def store(n):
        slot = lax.rem(n, SLOTS)
        row = pl.multiple_of(n * 2 * CHUNK, 2 * CHUNK)
        return pltpu.make_async_copy(stage.at[slot], out_ref.at[pl.ds(row, 2 * CHUNK), :], sems.at[slot])

    def step(n, carry):
        p = n // (chunks // PANELS)
        lanes = pl.ds(pl.multiple_of(lax.rem(n, chunks // PANELS) * CHUNK, CHUNK), CHUNK)
        amp = jnp.concatenate([b[p, :, lanes] for b in blocks], axis=0)
        prod = lax.dot_general(amp, lam_ref[p], (((0,), (0,)), ((), ())), preferred_element_type=jnp.float32)
        prod = prod * 0.5
        wide[pl.ds(0, CHUNK, 2), :] = prod[:, :LANES]
        wide[pl.ds(1, CHUNK, 2), :] = prod[:, LANES:]

        @pl.when(n >= SLOTS)
        def _():
            store(n - SLOTS).wait()

        stage[lax.rem(n, SLOTS)] = wide[...].astype(jnp.bfloat16)
        store(n).start()
        return carry

    lax.fori_loop(0, chunks, step, 0)
    for n in range(chunks - SLOTS, chunks):
        store(n).wait()
    part_copy.wait()


def vvvv_product(blocks, lam, part):
    vmem = pl.BlockSpec(memory_space=pltpu.VMEM)
    out, ovov = pl.pallas_call(
        vvvv_kernel,
        out_shape=(
            jax.ShapeDtypeStruct((PANELS * PANEL * PIECE * 2, LANES), jnp.bfloat16),
            jax.ShapeDtypeStruct(part.shape, part.dtype),
        ),
        in_specs=[vmem] * (NXY + 2),
        out_specs=(pl.BlockSpec(memory_space=pltpu.HBM),) * 2,
        scratch_shapes=[
            pltpu.VMEM((2 * CHUNK, LANES), jnp.float32),
            pltpu.VMEM((SLOTS, 2 * CHUNK, LANES), jnp.bfloat16),
            pltpu.SemaphoreType.DMA((SLOTS + 1,)),
        ],
        compiler_params=pltpu.CompilerParams(vmem_limit_bytes=24 * 2**20),
        name="vvvv_product",
    )(*blocks, lam, part)
    return out.reshape(PANELS, PANEL, PIECE, 2, LANES), ovov.reshape(PANELS, 2, OCC, OCC, PIECE)


def send(block, dy, dx):
    return lax.ppermute(block, "pair", pair_shift(dy, dx))


def after(value, *others):
    return lax.optimization_barrier((value,) + others)[0]


def shards(t2_amps, l2_amps, panel_start):
    amps = jnp.transpose(t2_amps[:, 0], (0, 2, 1))
    lams = jnp.transpose(l2_amps[:, 0], (0, 2, 1))
    place = jnp.stack([lax.axis_index("pair") // NZ, lax.axis_index("virt")]).astype(jnp.int32)
    parcel, own = cut(panel_start, amps, lams)
    near = lax.all_to_all(parcel, "pair", 0, 0, axis_index_groups=Z_GROUPS)

    there = send(own, 1, 0)
    plane = [own, there]
    for dx in X_SHIFTS:
        plane += [send(own, 0, dx), send(there, 0, dx)]
    near = after(near, *plane)

    held = to_rows(near)
    other = send(held, 1, 0)
    beside = {dx: send(held, 0, dx) for dx in X_SHIFTS}
    cross = {1: send(other, 0, 1), 3: send(other, 0, 3), 2: send(beside[2], 1, 0)}
    blocks = [held, other]
    for dx in X_SHIFTS:
        blocks += [beside[dx], cross[dx]]

    share = lax.all_to_all(plane_share(place, plane), "pair", 0, 0, axis_index_groups=Z_GROUPS)
    rows = after(pack(share), other)
    lam, part = lam_matrix(place, lax.all_gather(rows, "virt"))
    return vvvv_product(blocks, lam, part)


def solution(mesh):
    in_specs = (P(None, "pair", None, "virt"), P(None, "pair", None, "virt"), P())
    out_specs = (P(None, None, "virt", "pair", None), P(None, "pair", None, None, "virt"))
    return jax.shard_map(shards, mesh=mesh, in_specs=in_specs, out_specs=out_specs, check_vma=False)
```

```python
import functools

import jax
import jax.numpy as jnp
from jax import lax
from jax.experimental import pallas as pl
from jax.experimental.pallas import tpu as pltpu
from jax.sharding import PartitionSpec as P

NZ = 8
NX = 4
NY = 2
NXY = NX * NY
PAIRS = NZ * NXY
PANELS = 2
NV = 4
OCC = 4
PANEL = 128
PIECE = PANEL // NV
LANES = 128
VIRTUALS = 1600
WIDTH = VIRTUALS // NV
WINDOW = PIECE + 16
HEAD = VIRTUALS // LANES * LANES
LAST = (VIRTUALS - WIDTH) // LANES * LANES
AMP_ROWS = PANELS * OCC * PIECE
LAM_ROWS = PANELS * PANEL
Z_GROUPS = [[xy * NZ + z for z in range(NZ)] for xy in range(NXY)]
X_SHIFTS = (1, 3, 2)
HALF = AMP_ROWS // PANELS
PART_ROWS = 64
OWN_ROWS = NXY * PANELS * 2


def pair_shift(dy, dx):
    return [
        ((y * NX + x) * NZ + z, (((y + dy) % NY) * NX + (x + dx) % NX) * NZ + z)
        for y in range(NY)
        for x in range(NX)
        for z in range(NZ)
    ]


def cut_kernel(start_ref, amp_ref, lam_ref, line_ref, own_ref, buf, rows, last, flip, sems):
    copies = []
    for a, src in enumerate((amp_ref, lam_ref)):
        for p in range(PANELS):
            base = jnp.minimum(start_ref[p] // 16 * 16, WIDTH - WINDOW)
            base = pl.multiple_of(base, 16)
            copy = pltpu.make_async_copy(
                src.at[:, pl.ds(base, WINDOW), :], buf.at[a, p], sems.at[a, p]
            )
            copy.start()
            copies.append((a, p, copy))
    lane = lax.broadcasted_iota(jnp.int32, (OCC * PIECE, LANES), 1)
    for a, p, copy in copies:
        start = start_ref[p]
        offset = start - jnp.minimum(start // 16 * 16, WIDTH - WINDOW)
        copy.wait()
        for i in range(OCC):
            tail = buf[a, p, i, :, HEAD:].astype(jnp.float32)
            blank = jnp.zeros((WINDOW, HEAD + LANES - VIRTUALS), jnp.float32)
            last[i, :, : HEAD - LAST] = buf[a, p, i, :, LAST:HEAD].astype(jnp.float32)
            last[i, :, HEAD - LAST : HEAD - LAST + LANES] = jnp.concatenate([tail, blank], axis=1)
        mine = jnp.zeros((OCC * PIECE, LANES), jnp.float32)
        for m in range(NV):
            column = m * WIDTH + start
            tile = column // LANES
            shift = lax.rem(m * PIECE + LANES - lax.rem(column, LANES), LANES)
            for half in range(2):
                if m < NV - 1:
                    lanes = pl.ds(pl.multiple_of((tile + half) * LANES, LANES), LANES)
                    rows[...] = buf[a, p, :, :, lanes].astype(jnp.float32)
                else:
                    lanes = pl.ds(pl.multiple_of((tile + half) * LANES - LAST, LANES), LANES)
                    rows[...] = last[:, :, lanes]
                parts = [rows[i, pl.ds(offset, PIECE), :] for i in range(OCC)]
                turned = pltpu.roll(jnp.concatenate(parts, axis=0), shift, 1)
                first = lax.rem(column, LANES)
                inside = (lane >= m * PIECE) & (lane < (m + 1) * PIECE)
                here = lane - m * PIECE + first
                inside = inside & ((here < LANES) if half == 0 else (here >= LANES))
                mine = jnp.where(inside, turned, mine)
        turned = mine.T
        if a == 0:
            flip[...] = turned
            for i in range(OCC):
                cells = [flip[pl.ds(q, PIECE, 4), :][:, PIECE * i : PIECE * (i + 1)] for q in range(4)]
                block = jnp.concatenate(cells, axis=1).astype(jnp.bfloat16)
                own_ref[pl.ds((p * OCC + i) * PIECE, PIECE), :] = block
                for z in range(NZ):
                    line_ref[z, pl.ds((p * OCC + i) * PIECE, PIECE), :] = block
        else:
            own_ref[pl.ds(AMP_ROWS + p * PANEL, PANEL), :] = turned.astype(jnp.bfloat16)


def cut(panel_start, amps, lams):
    return pl.pallas_call(
        cut_kernel,
        out_shape=(
            jax.ShapeDtypeStruct((NZ, AMP_ROWS, LANES), jnp.bfloat16),
            jax.ShapeDtypeStruct((AMP_ROWS + LAM_ROWS, LANES), jnp.bfloat16),
        ),
        in_specs=[
            pl.BlockSpec(memory_space=pltpu.SMEM),
            pl.BlockSpec(memory_space=pltpu.HBM),
            pl.BlockSpec(memory_space=pltpu.HBM),
        ],
        out_specs=(pl.BlockSpec(memory_space=pltpu.VMEM),) * 2,
        scratch_shapes=[
            pltpu.VMEM((2, PANELS, OCC, WINDOW, VIRTUALS), jnp.bfloat16),
            pltpu.VMEM((OCC, WINDOW, LANES), jnp.float32),
            pltpu.VMEM((OCC, WINDOW, HEAD - LAST + 2 * LANES), jnp.float32),
            pltpu.VMEM((LANES, LANES), jnp.float32),
            pltpu.SemaphoreType.DMA((2, PANELS)),
        ],
        compiler_params=pltpu.CompilerParams(vmem_limit_bytes=56 * 2**20),
        name="cut_panels",
    )(panel_start, amps, lams)


def rows_kernel(near_ref, out_ref, wide):
    for p in range(PANELS):
        for k in range(NZ):
            part = near_ref[k, pl.ds(p * HALF, HALF), :]
            wide[pl.ds(k * HALF, HALF), :] = part.astype(jnp.float32)
        for r in range(PIECE):
            out_ref[p, :, pl.ds(r * LANES, LANES)] = wide[pl.ds(r, NZ * OCC, PIECE), :].astype(jnp.bfloat16)


def to_rows(near):
    vmem = pl.BlockSpec(memory_space=pltpu.VMEM)
    return pl.pallas_call(
        rows_kernel,
        out_shape=jax.ShapeDtypeStruct((PANELS, NZ * OCC, PIECE * LANES), jnp.bfloat16),
        in_specs=[vmem],
        out_specs=vmem,
        scratch_shapes=[pltpu.VMEM((NZ * HALF, LANES), jnp.float32)],
        compiler_params=pltpu.CompilerParams(vmem_limit_bytes=16 * 2**20),
        name="occupied_rows",
    )(near)


def plane_kernel(place_ref, *refs):
    ins, out_ref, pick, prod, wide, own = refs[:NXY], *refs[NXY:]
    xy = place_ref[0]
    lane = lax.broadcasted_iota(jnp.int32, (OCC * 4, LANES), 1) // PIECE
    for p in range(PANELS):
        for s in range(NXY):
            wide[...] = ins[s][pl.ds(p * HALF, HALF), :].astype(jnp.float32)
            amp = jnp.concatenate([wide[pl.ds(j * PIECE + 4 * xy, 4), :] for j in range(OCC)], axis=0)
            for d in range(4):
                turned = amp if d == 0 else pltpu.roll(amp, PIECE * d, 1)
                for i in range(OCC):
                    row = (i - d) % 4 * 64 + i * 16
                    pick[pl.ds(row, 16), pl.ds(s * LANES, LANES)] = jnp.where(lane == i, turned, 0.0).astype(jnp.bfloat16)
            row = pl.multiple_of(AMP_ROWS + p * PANEL + 16 * xy, 16)
            own[s, p] = ins[s][pl.ds(row, 16), :].astype(jnp.float32)
        lam = jnp.concatenate([ins[s][pl.ds(AMP_ROWS + p * PANEL, PANEL), :] for s in range(NXY)], axis=1)
        prod[...] = lax.dot_general(pick[...], lam, (((1,), (1,)), ((), ())), preferred_element_type=jnp.float32)
        for z in range(NZ):
            for beta in range(2):
                for j in range(OCC):
                    row = (z % 2 * 2 + beta) * 64 + j * 4 + z // 2
                    out_ref[z, pl.ds(p * 32 + beta * 16 + j * 4, OCC), :] = prod[pl.ds(row, OCC, 16), :]
    for z in range(NZ):
        for s in range(NXY):
            for p in range(PANELS):
                out_ref[z, pl.ds(PART_ROWS + s * 4 + p * 2, 2), :] = own[s, p, pl.ds(2 * z, 2), :]


def plane_share(place, parts):
    vmem = pl.BlockSpec(memory_space=pltpu.VMEM)
    return pl.pallas_call(
        plane_kernel,
        out_shape=jax.ShapeDtypeStruct((NZ, PART_ROWS + OWN_ROWS, LANES), jnp.float32),
        in_specs=[pl.BlockSpec(memory_space=pltpu.SMEM)] + [vmem] * NXY,
        out_specs=vmem,
        scratch_shapes=[
            pltpu.VMEM((2 * LANES, NXY * LANES), jnp.bfloat16),
            pltpu.VMEM((2 * LANES, LANES), jnp.float32),
            pltpu.VMEM((HALF, LANES), jnp.float32),
            pltpu.VMEM((NXY, PANELS, 16, LANES), jnp.float32),
        ],
        compiler_params=pltpu.CompilerParams(vmem_limit_bytes=16 * 2**20),
        name="plane_share",
    )(place, *parts)


def pack_kernel(in_ref, out_ref, rows):
    total = in_ref[0, pl.ds(0, PART_ROWS), :]
    for z in range(1, NZ):
        total = total + in_ref[z, pl.ds(0, PART_ROWS), :]
    for z in range(NZ):
        for s in range(NXY):
            rows[pl.ds((s * NZ + z) * 4, 4), :] = in_ref[z, pl.ds(PART_ROWS + s * 4, 4), :]
    out_ref[pl.ds(0, NZ * OWN_ROWS), :] = rows[...].astype(jnp.bfloat16)
    high = total.astype(jnp.bfloat16)
    out_ref[pl.ds(NZ * OWN_ROWS, PART_ROWS), :] = high
    out_ref[pl.ds(NZ * OWN_ROWS + PART_ROWS, PART_ROWS), :] = (total - high.astype(jnp.float32)).astype(jnp.bfloat16)


def pack(got):
    vmem = pl.BlockSpec(memory_space=pltpu.VMEM)
    return pl.pallas_call(
        pack_kernel,
        out_shape=jax.ShapeDtypeStruct((NZ * OWN_ROWS + 2 * PART_ROWS, LANES), jnp.bfloat16),
        in_specs=[vmem],
        out_specs=vmem,
        scratch_shapes=[pltpu.VMEM((NZ * OWN_ROWS, LANES), jnp.float32)],
        compiler_params=pltpu.CompilerParams(vmem_limit_bytes=8 * 2**20),
        name="pack_shares",
    )(got)


def lam_kernel(place_ref, own_ref, line_ref, part_ref, wide, rows):
    lane = lax.broadcasted_iota(jnp.int32, (NXY * NZ, LANES), 1) // PIECE
    count = NXY * OWN_ROWS
    wide[...] = own_ref[:, pl.ds(0, count), :].astype(jnp.float32)
    for p in range(PANELS):
        for g in range(2):
            parts = [wide[v, pl.ds(2 * p + g, NXY * NZ, 4), :] for v in range(NV)]
            for i in range(OCC):
                cell = jnp.zeros((NXY * NZ, LANES), jnp.float32)
                for v in range(NV):
                    turn = PIECE * ((v - i) % 4)
                    part = parts[v] if turn == 0 else pltpu.roll(parts[v], turn, 1)
                    cell = jnp.where(lane == v, part, cell)
                rows[pl.ds(i, NXY * NZ, OCC), :] = cell
            line_ref[p, :, pl.ds(g * LANES, LANES)] = rows[...].astype(jnp.bfloat16)
    total = jnp.zeros((PART_ROWS, LANES), jnp.float32)
    for v in range(NV):
        for n in range(2):
            total = total + own_ref[v, pl.ds(count + n * PART_ROWS, PART_ROWS), :].astype(jnp.float32)
    mine = pltpu.roll(-total, lax.rem(LANES - place_ref[1] * PIECE, LANES), 1)
    part_ref[...] = mine[:, :PIECE].astype(jnp.bfloat16)


def lam_matrix(place, own):
    vmem = pl.BlockSpec(memory_space=pltpu.VMEM)
    matrix = jax.ShapeDtypeStruct((PANELS, PAIRS * OCC, 2 * LANES), jnp.bfloat16)
    return pl.pallas_call(
        lam_kernel,
        out_shape=(matrix, jax.ShapeDtypeStruct((PART_ROWS, PIECE), jnp.bfloat16)),
        in_specs=[pl.BlockSpec(memory_space=pltpu.SMEM), vmem],
        out_specs=(vmem, vmem),
        scratch_shapes=[
            pltpu.VMEM((NV, NXY * OWN_ROWS, LANES), jnp.float32),
            pltpu.VMEM((PAIRS * OCC, LANES), jnp.float32),
        ],
        compiler_params=pltpu.CompilerParams(vmem_limit_bytes=16 * 2**20),
        name="lam_matrix",
    )(place, own)


CHUNK = 2048
SLOTS = 2


def vvvv_kernel(*refs):
    blocks, lam_ref, part_ref, out_ref, ovov_ref, wide, stage, late, sems = refs[:NXY], *refs[NXY:]
    part_copy = pltpu.make_async_copy(part_ref, ovov_ref, sems.at[SLOTS])
    part_copy.start()
    chunks = PANELS * PIECE * LANES // CHUNK

    def fetch(n, p):
        return pltpu.make_async_copy(blocks[3 + 2 * n].at[p], late.at[p, n], sems.at[SLOTS + 1 + 3 * p + n])

    for p in range(PANELS):
        for n in range(3):
            fetch(n, p).start()

    def store(n):
        slot = lax.rem(n, SLOTS)
        row = pl.multiple_of(n * 2 * CHUNK, 2 * CHUNK)
        return pltpu.make_async_copy(stage.at[slot], out_ref.at[pl.ds(row, 2 * CHUNK), :], sems.at[slot])

    def step(n, carry):
        p = n // (chunks // PANELS)
        lanes = pl.ds(pl.multiple_of(lax.rem(n, chunks // PANELS) * CHUNK, CHUNK), CHUNK)

        @pl.when(lax.rem(n, chunks // PANELS) == 0)
        def _():
            for m in range(3):
                fetch(m, p).wait()

        parts = [late[p, (s - 3) // 2, :, lanes] if s in (3, 5, 7) else blocks[s][p, :, lanes] for s in range(NXY)]
        amp = jnp.concatenate(parts, axis=0)
        prod = lax.dot_general(amp, lam_ref[p], (((0,), (0,)), ((), ())), preferred_element_type=jnp.float32)
        prod = prod * 0.5
        wide[pl.ds(0, CHUNK, 2), :] = prod[:, :LANES]
        wide[pl.ds(1, CHUNK, 2), :] = prod[:, LANES:]

        @pl.when(n >= SLOTS)
        def _():
            store(n - SLOTS).wait()

        stage[lax.rem(n, SLOTS)] = wide[...].astype(jnp.bfloat16)
        store(n).start()
        return carry

    lax.fori_loop(0, chunks, step, 0)
    for n in range(chunks - SLOTS, chunks):
        store(n).wait()
    part_copy.wait()


def vvvv_product(blocks, lam, part):
    vmem = pl.BlockSpec(memory_space=pltpu.VMEM)
    out, ovov = pl.pallas_call(
        vvvv_kernel,
        out_shape=(
            jax.ShapeDtypeStruct((PANELS * PANEL * PIECE * 2, LANES), jnp.bfloat16),
            jax.ShapeDtypeStruct(part.shape, part.dtype),
        ),
        in_specs=[pl.BlockSpec(memory_space=pl.ANY) if s in (3, 5, 7) else vmem for s in range(NXY)] + [vmem] * 2,
        out_specs=(pl.BlockSpec(memory_space=pltpu.HBM),) * 2,
        scratch_shapes=[
            pltpu.VMEM((2 * CHUNK, LANES), jnp.float32),
            pltpu.VMEM((SLOTS, 2 * CHUNK, LANES), jnp.bfloat16),
            pltpu.VMEM((PANELS, 3, NZ * OCC, PIECE * LANES), jnp.bfloat16),
            pltpu.SemaphoreType.DMA((SLOTS + 1 + 3 * PANELS,)),
        ],
        compiler_params=pltpu.CompilerParams(vmem_limit_bytes=24 * 2**20),
        name="vvvv_product",
    )(*blocks, lam, part)
    return out.reshape(PANELS, PANEL, PIECE, 2, LANES), ovov.reshape(PANELS, 2, OCC, OCC, PIECE)


def send(block, dy, dx):
    return lax.ppermute(block, "pair", pair_shift(dy, dx))


def after(value, *others):
    return lax.optimization_barrier((value,) + others)[0]


def shards(t2_amps, l2_amps, panel_start):
    amps = jnp.transpose(t2_amps[:, 0], (0, 2, 1))
    lams = jnp.transpose(l2_amps[:, 0], (0, 2, 1))
    place = jnp.stack([lax.axis_index("pair") // NZ, lax.axis_index("virt")]).astype(jnp.int32)
    parcel, own = cut(panel_start, amps, lams)
    near = lax.all_to_all(parcel, "pair", 0, 0, axis_index_groups=Z_GROUPS)

    there = send(own, 1, 0)
    plane = [own, there]
    for dx in X_SHIFTS:
        plane += [send(own, 0, dx), send(there, 0, dx)]
    near = after(near, *plane)

    held = to_rows(near)
    other = send(held, 1, 0)
    beside = {dx: send(held, 0, dx) for dx in X_SHIFTS}
    cross = {1: send(other, 0, 1), 3: send(other, 0, 3), 2: send(beside[2], 1, 0)}
    blocks = [held, other]
    for dx in X_SHIFTS:
        blocks += [beside[dx], cross[dx]]

    share = lax.all_to_all(plane_share(place, plane), "pair", 0, 0, axis_index_groups=Z_GROUPS)
    rows = after(pack(share), other)
    lam, part = lam_matrix(place, lax.all_gather(rows, "virt"))
    return vvvv_product(blocks, lam, part)


def solution(mesh):
    in_specs = (P(None, "pair", None, "virt"), P(None, "pair", None, "virt"), P())
    out_specs = (P(None, None, "virt", "pair", None), P(None, "pair", None, None, "virt"))
    return jax.shard_map(shards, mesh=mesh, in_specs=in_specs, out_specs=out_specs, check_vma=False)
```

```python
import functools

import jax
import jax.numpy as jnp
from jax import lax
from jax.experimental import pallas as pl
from jax.experimental.pallas import tpu as pltpu
from jax.sharding import PartitionSpec as P

NZ = 8
NX = 4
NY = 2
NXY = NX * NY
PAIRS = NZ * NXY
PANELS = 2
NV = 4
OCC = 4
PANEL = 128
PIECE = PANEL // NV
LANES = 128
VIRTUALS = 1600
WIDTH = VIRTUALS // NV
WINDOW = PIECE + 16
HEAD = VIRTUALS // LANES * LANES
LAST = (VIRTUALS - WIDTH) // LANES * LANES
AMP_ROWS = PANELS * OCC * PIECE
LAM_ROWS = PANELS * PANEL
Z_GROUPS = [[xy * NZ + z for z in range(NZ)] for xy in range(NXY)]
X_SHIFTS = (1, 3, 2)
HALF = AMP_ROWS // PANELS
PART_ROWS = 64
OWN_ROWS = NXY * PANELS * 2


def pair_shift(dy, dx):
    return [
        ((y * NX + x) * NZ + z, (((y + dy) % NY) * NX + (x + dx) % NX) * NZ + z)
        for y in range(NY)
        for x in range(NX)
        for z in range(NZ)
    ]


def cut_kernel(start_ref, amp_ref, lam_ref, line_ref, own_ref, buf, rows, last, flip, sems):
    copies = []
    for a, src in enumerate((amp_ref, lam_ref)):
        for p in range(PANELS):
            base = jnp.minimum(start_ref[p] // 16 * 16, WIDTH - WINDOW)
            base = pl.multiple_of(base, 16)
            copy = pltpu.make_async_copy(
                src.at[:, pl.ds(base, WINDOW), :], buf.at[a, p], sems.at[a, p]
            )
            copy.start()
            copies.append((a, p, copy))
    lane = lax.broadcasted_iota(jnp.int32, (OCC * PIECE, LANES), 1)
    for a, p, copy in copies:
        start = start_ref[p]
        offset = start - jnp.minimum(start // 16 * 16, WIDTH - WINDOW)
        copy.wait()
        for i in range(OCC):
            tail = buf[a, p, i, :, HEAD:].astype(jnp.float32)
            blank = jnp.zeros((WINDOW, HEAD + LANES - VIRTUALS), jnp.float32)
            last[i, :, : HEAD - LAST] = buf[a, p, i, :, LAST:HEAD].astype(jnp.float32)
            last[i, :, HEAD - LAST : HEAD - LAST + LANES] = jnp.concatenate([tail, blank], axis=1)
        mine = jnp.zeros((OCC * PIECE, LANES), jnp.float32)
        for m in range(NV):
            column = m * WIDTH + start
            tile = column // LANES
            shift = lax.rem(m * PIECE + LANES - lax.rem(column, LANES), LANES)
            for half in range(2):
                if m < NV - 1:
                    lanes = pl.ds(pl.multiple_of((tile + half) * LANES, LANES), LANES)
                    rows[...] = buf[a, p, :, :, lanes].astype(jnp.float32)
                else:
                    lanes = pl.ds(pl.multiple_of((tile + half) * LANES - LAST, LANES), LANES)
                    rows[...] = last[:, :, lanes]
                parts = [rows[i, pl.ds(offset, PIECE), :] for i in range(OCC)]
                turned = pltpu.roll(jnp.concatenate(parts, axis=0), shift, 1)
                first = lax.rem(column, LANES)
                inside = (lane >= m * PIECE) & (lane < (m + 1) * PIECE)
                here = lane - m * PIECE + first
                inside = inside & ((here < LANES) if half == 0 else (here >= LANES))
                mine = jnp.where(inside, turned, mine)
        turned = mine.T
        if a == 0:
            flip[...] = turned
            for i in range(OCC):
                cells = [flip[pl.ds(q, PIECE, 4), :][:, PIECE * i : PIECE * (i + 1)] for q in range(4)]
                block = jnp.concatenate(cells, axis=1).astype(jnp.bfloat16)
                own_ref[pl.ds((p * OCC + i) * PIECE, PIECE), :] = block
                for z in range(NZ):
                    line_ref[z, pl.ds((p * OCC + i) * PIECE, PIECE), :] = block
        else:
            own_ref[pl.ds(AMP_ROWS + p * PANEL, PANEL), :] = turned.astype(jnp.bfloat16)


def cut(panel_start, amps, lams):
    return pl.pallas_call(
        cut_kernel,
        out_shape=(
            jax.ShapeDtypeStruct((NZ, AMP_ROWS, LANES), jnp.bfloat16),
            jax.ShapeDtypeStruct((AMP_ROWS + LAM_ROWS, LANES), jnp.bfloat16),
        ),
        in_specs=[
            pl.BlockSpec(memory_space=pltpu.SMEM),
            pl.BlockSpec(memory_space=pltpu.HBM),
            pl.BlockSpec(memory_space=pltpu.HBM),
        ],
        out_specs=(pl.BlockSpec(memory_space=pltpu.VMEM),) * 2,
        scratch_shapes=[
            pltpu.VMEM((2, PANELS, OCC, WINDOW, VIRTUALS), jnp.bfloat16),
            pltpu.VMEM((OCC, WINDOW, LANES), jnp.float32),
            pltpu.VMEM((OCC, WINDOW, HEAD - LAST + 2 * LANES), jnp.float32),
            pltpu.VMEM((LANES, LANES), jnp.float32),
            pltpu.SemaphoreType.DMA((2, PANELS)),
        ],
        compiler_params=pltpu.CompilerParams(vmem_limit_bytes=56 * 2**20),
        name="cut_panels",
    )(panel_start, amps, lams)


def rows_kernel(near_ref, out_ref, wide):
    for p in range(PANELS):
        for k in range(NZ):
            part = near_ref[k, pl.ds(p * HALF, HALF), :]
            wide[pl.ds(k * HALF, HALF), :] = part.astype(jnp.float32)
        for r in range(PIECE):
            out_ref[p, :, pl.ds(r * LANES, LANES)] = wide[pl.ds(r, NZ * OCC, PIECE), :].astype(jnp.bfloat16)


def to_rows(near):
    vmem = pl.BlockSpec(memory_space=pltpu.VMEM)
    return pl.pallas_call(
        rows_kernel,
        out_shape=jax.ShapeDtypeStruct((PANELS, NZ * OCC, PIECE * LANES), jnp.bfloat16),
        in_specs=[vmem],
        out_specs=vmem,
        scratch_shapes=[pltpu.VMEM((NZ * HALF, LANES), jnp.float32)],
        compiler_params=pltpu.CompilerParams(vmem_limit_bytes=16 * 2**20),
        name="occupied_rows",
    )(near)


def plane_kernel(place_ref, *refs):
    ins, out_ref, pick, prod, wide, own = refs[:NXY], *refs[NXY:]
    xy = place_ref[0]
    lane = lax.broadcasted_iota(jnp.int32, (OCC * 4, LANES), 1) // PIECE
    for p in range(PANELS):
        for s in range(NXY):
            wide[...] = ins[s][pl.ds(p * HALF, HALF), :].astype(jnp.float32)
            amp = jnp.concatenate([wide[pl.ds(j * PIECE + 4 * xy, 4), :] for j in range(OCC)], axis=0)
            for d in range(4):
                turned = amp if d == 0 else pltpu.roll(amp, PIECE * d, 1)
                for i in range(OCC):
                    row = (i - d) % 4 * 64 + i * 16
                    pick[pl.ds(row, 16), pl.ds(s * LANES, LANES)] = jnp.where(lane == i, turned, 0.0).astype(jnp.bfloat16)
            row = pl.multiple_of(AMP_ROWS + p * PANEL + 16 * xy, 16)
            own[s, p] = ins[s][pl.ds(row, 16), :].astype(jnp.float32)
        lam = jnp.concatenate([ins[s][pl.ds(AMP_ROWS + p * PANEL, PANEL), :] for s in range(NXY)], axis=1)
        prod[...] = lax.dot_general(pick[...], lam, (((1,), (1,)), ((), ())), preferred_element_type=jnp.float32)
        for z in range(NZ):
            for beta in range(2):
                for j in range(OCC):
                    row = (z % 2 * 2 + beta) * 64 + j * 4 + z // 2
                    out_ref[z, pl.ds(p * 32 + beta * 16 + j * 4, OCC), :] = prod[pl.ds(row, OCC, 16), :]
    for z in range(NZ):
        for s in range(NXY):
            for p in range(PANELS):
                out_ref[z, pl.ds(PART_ROWS + s * 4 + p * 2, 2), :] = own[s, p, pl.ds(2 * z, 2), :]


def plane_share(place, parts):
    vmem = pl.BlockSpec(memory_space=pltpu.VMEM)
    return pl.pallas_call(
        plane_kernel,
        out_shape=jax.ShapeDtypeStruct((NZ, PART_ROWS + OWN_ROWS, LANES), jnp.float32),
        in_specs=[pl.BlockSpec(memory_space=pltpu.SMEM)] + [vmem] * NXY,
        out_specs=vmem,
        scratch_shapes=[
            pltpu.VMEM((2 * LANES, NXY * LANES), jnp.bfloat16),
            pltpu.VMEM((2 * LANES, LANES), jnp.float32),
            pltpu.VMEM((HALF, LANES), jnp.float32),
            pltpu.VMEM((NXY, PANELS, 16, LANES), jnp.float32),
        ],
        compiler_params=pltpu.CompilerParams(vmem_limit_bytes=16 * 2**20),
        name="plane_share",
    )(place, *parts)


def pack_kernel(in_ref, out_ref, rows):
    total = in_ref[0, pl.ds(0, PART_ROWS), :]
    for z in range(1, NZ):
        total = total + in_ref[z, pl.ds(0, PART_ROWS), :]
    for z in range(NZ):
        for s in range(NXY):
            rows[pl.ds((s * NZ + z) * 4, 4), :] = in_ref[z, pl.ds(PART_ROWS + s * 4, 4), :]
    out_ref[pl.ds(0, NZ * OWN_ROWS), :] = rows[...].astype(jnp.bfloat16)
    high = total.astype(jnp.bfloat16)
    out_ref[pl.ds(NZ * OWN_ROWS, PART_ROWS), :] = high
    out_ref[pl.ds(NZ * OWN_ROWS + PART_ROWS, PART_ROWS), :] = (total - high.astype(jnp.float32)).astype(jnp.bfloat16)


def pack(got):
    vmem = pl.BlockSpec(memory_space=pltpu.VMEM)
    return pl.pallas_call(
        pack_kernel,
        out_shape=jax.ShapeDtypeStruct((NZ * OWN_ROWS + 2 * PART_ROWS, LANES), jnp.bfloat16),
        in_specs=[vmem],
        out_specs=vmem,
        scratch_shapes=[pltpu.VMEM((NZ * OWN_ROWS, LANES), jnp.float32)],
        compiler_params=pltpu.CompilerParams(vmem_limit_bytes=8 * 2**20),
        name="pack_shares",
    )(got)


def lam_kernel(place_ref, own_ref, line_ref, part_ref, wide, rows):
    lane = lax.broadcasted_iota(jnp.int32, (NXY * NZ, LANES), 1) // PIECE
    count = NXY * OWN_ROWS
    wide[...] = own_ref[:, pl.ds(0, count), :].astype(jnp.float32)
    for p in range(PANELS):
        for g in range(2):
            parts = [wide[v, pl.ds(2 * p + g, NXY * NZ, 4), :] for v in range(NV)]
            for i in range(OCC):
                cell = jnp.zeros((NXY * NZ, LANES), jnp.float32)
                for v in range(NV):
                    turn = PIECE * ((v - i) % 4)
                    part = parts[v] if turn == 0 else pltpu.roll(parts[v], turn, 1)
                    cell = jnp.where(lane == v, part, cell)
                rows[pl.ds(i, NXY * NZ, OCC), :] = cell
            line_ref[p, :, pl.ds(g * LANES, LANES)] = rows[...].astype(jnp.bfloat16)
    total = jnp.zeros((PART_ROWS, LANES), jnp.float32)
    for v in range(NV):
        for n in range(2):
            total = total + own_ref[v, pl.ds(count + n * PART_ROWS, PART_ROWS), :].astype(jnp.float32)
    mine = pltpu.roll(-total, lax.rem(LANES - place_ref[1] * PIECE, LANES), 1)
    part_ref[...] = mine[:, :PIECE].astype(jnp.bfloat16)


def lam_matrix(place, own):
    vmem = pl.BlockSpec(memory_space=pltpu.VMEM)
    matrix = jax.ShapeDtypeStruct((PANELS, PAIRS * OCC, 2 * LANES), jnp.bfloat16)
    return pl.pallas_call(
        lam_kernel,
        out_shape=(matrix, jax.ShapeDtypeStruct((PART_ROWS, PIECE), jnp.bfloat16)),
        in_specs=[pl.BlockSpec(memory_space=pltpu.SMEM), vmem],
        out_specs=(vmem, vmem),
        scratch_shapes=[
            pltpu.VMEM((NV, NXY * OWN_ROWS, LANES), jnp.float32),
            pltpu.VMEM((PAIRS * OCC, LANES), jnp.float32),
        ],
        compiler_params=pltpu.CompilerParams(vmem_limit_bytes=16 * 2**20),
        name="lam_matrix",
    )(place, own)


CHUNK = 2048
SLOTS = 2


def vvvv_kernel(*refs):
    blocks, lam_ref, part_ref, out_ref, ovov_ref, wide, stage, late, sems = refs[:NXY], *refs[NXY:]
    part_copy = pltpu.make_async_copy(part_ref, ovov_ref, sems.at[SLOTS])
    part_copy.start()
    chunks = PANELS * PIECE * LANES // CHUNK

    def fetch(n, p):
        return pltpu.make_async_copy(blocks[3 + 2 * n].at[p], late.at[p, n], sems.at[SLOTS + 1 + 3 * p + n])

    for p in range(PANELS):
        for n in range(3):
            fetch(n, p).start()

    def store(n):
        slot = lax.rem(n, SLOTS)
        row = pl.multiple_of(n * 2 * CHUNK, 2 * CHUNK)
        return pltpu.make_async_copy(stage.at[slot], out_ref.at[pl.ds(row, 2 * CHUNK), :], sems.at[slot])

    def step(n, carry):
        p = n // (chunks // PANELS)
        lanes = pl.ds(pl.multiple_of(lax.rem(n, chunks // PANELS) * CHUNK, CHUNK), CHUNK)

        @pl.when(lax.rem(n, chunks // PANELS) == 0)
        def _():
            for m in range(3):
                fetch(m, p).wait()

        parts = [late[p, (s - 3) // 2, :, lanes] if s in (3, 5, 7) else blocks[s][p, :, lanes] for s in range(NXY)]
        amp = jnp.concatenate(parts, axis=0)
        prod = lax.dot_general(amp, lam_ref[p], (((0,), (0,)), ((), ())), preferred_element_type=jnp.float32)
        prod = prod * 0.5
        wide[pl.ds(0, CHUNK, 2), :] = prod[:, :LANES]
        wide[pl.ds(1, CHUNK, 2), :] = prod[:, LANES:]

        @pl.when(n >= SLOTS)
        def _():
            store(n - SLOTS).wait()

        stage[lax.rem(n, SLOTS)] = wide[...].astype(jnp.bfloat16)
        store(n).start()
        return carry

    lax.fori_loop(0, chunks, step, 0)
    for n in range(chunks - SLOTS, chunks):
        store(n).wait()
    part_copy.wait()


def vvvv_product(blocks, lam, part):
    vmem = pl.BlockSpec(memory_space=pltpu.VMEM)
    out, ovov = pl.pallas_call(
        vvvv_kernel,
        out_shape=(
            jax.ShapeDtypeStruct((PANELS * PANEL * PIECE * 2, LANES), jnp.bfloat16),
            jax.ShapeDtypeStruct(part.shape, part.dtype),
        ),
        in_specs=[pl.BlockSpec(memory_space=pl.ANY) if s in (3, 5, 7) else vmem for s in range(NXY)] + [vmem] * 2,
        out_specs=(pl.BlockSpec(memory_space=pltpu.HBM),) * 2,
        scratch_shapes=[
            pltpu.VMEM((2 * CHUNK, LANES), jnp.float32),
            pltpu.VMEM((SLOTS, 2 * CHUNK, LANES), jnp.bfloat16),
            pltpu.VMEM((PANELS, 3, NZ * OCC, PIECE * LANES), jnp.bfloat16),
            pltpu.SemaphoreType.DMA((SLOTS + 1 + 3 * PANELS,)),
        ],
        compiler_params=pltpu.CompilerParams(vmem_limit_bytes=24 * 2**20),
        name="vvvv_product",
    )(*blocks, lam, part)
    return out.reshape(PANELS, PANEL, PIECE, 2, LANES), ovov.reshape(PANELS, 2, OCC, OCC, PIECE)


def send(block, dy, dx):
    return lax.ppermute(block, "pair", pair_shift(dy, dx))


def after(value, *others):
    return lax.optimization_barrier((value,) + others)[0]


def shards(t2_amps, l2_amps, panel_start):
    amps = jnp.transpose(t2_amps[:, 0], (0, 2, 1))
    lams = jnp.transpose(l2_amps[:, 0], (0, 2, 1))
    place = jnp.stack([lax.axis_index("pair") // NZ, lax.axis_index("virt")]).astype(jnp.int32)
    parcel, own = cut(panel_start, amps, lams)
    near = lax.all_to_all(parcel, "pair", 0, 0, axis_index_groups=Z_GROUPS)

    there = send(own, 1, 0)
    plane = [own, there]
    for dx in X_SHIFTS:
        near_own = send(own, 0, dx)
        plane += [near_own, send(near_own, 1, 0) if dx == 2 else send(there, 0, dx)]
    near = after(near, *plane)

    held = to_rows(near)
    other = send(held, 1, 0)
    beside = {dx: send(held, 0, dx) for dx in X_SHIFTS}
    cross = {1: send(other, 0, 1), 3: send(other, 0, 3), 2: send(beside[2], 1, 0)}
    blocks = [held, other]
    for dx in X_SHIFTS:
        blocks += [beside[dx], cross[dx]]

    share = lax.all_to_all(plane_share(place, plane), "pair", 0, 0, axis_index_groups=Z_GROUPS)
    rows = after(pack(share), other)
    lam, part = lam_matrix(place, lax.all_gather(rows, "virt"))
    return vvvv_product(blocks, lam, part)


def solution(mesh):
    in_specs = (P(None, "pair", None, "virt"), P(None, "pair", None, "virt"), P())
    out_specs = (P(None, None, "virt", "pair", None), P(None, "pair", None, None, "virt"))
    return jax.shard_map(shards, mesh=mesh, in_specs=in_specs, out_specs=out_specs, check_vma=False)
```

```python
import functools

import jax
import jax.numpy as jnp
from jax import lax
from jax.experimental import pallas as pl
from jax.experimental.pallas import tpu as pltpu
from jax.sharding import PartitionSpec as P

NZ = 8
NX = 4
NY = 2
NXY = NX * NY
PAIRS = NZ * NXY
PANELS = 2
NV = 4
OCC = 4
PANEL = 128
PIECE = PANEL // NV
LANES = 128
VIRTUALS = 1600
WIDTH = VIRTUALS // NV
WINDOW = PIECE + 16
HEAD = VIRTUALS // LANES * LANES
LAST = (VIRTUALS - WIDTH) // LANES * LANES
AMP_ROWS = PANELS * OCC * PIECE
LAM_ROWS = PANELS * PANEL
Z_GROUPS = [[xy * NZ + z for z in range(NZ)] for xy in range(NXY)]
X_SHIFTS = (1, 3, 2)
HALF = AMP_ROWS // PANELS
PART_ROWS = 64
OWN_ROWS = NXY * PANELS * 2


def pair_shift(dy, dx):
    return [
        ((y * NX + x) * NZ + z, (((y + dy) % NY) * NX + (x + dx) % NX) * NZ + z)
        for y in range(NY)
        for x in range(NX)
        for z in range(NZ)
    ]


def cut_kernel(start_ref, amp_ref, lam_ref, line_ref, own_ref, buf, rows, last, flip, sems):
    copies = []
    for a, src in enumerate((amp_ref, lam_ref)):
        for p in range(PANELS):
            base = jnp.minimum(start_ref[p] // 16 * 16, WIDTH - WINDOW)
            base = pl.multiple_of(base, 16)
            copy = pltpu.make_async_copy(
                src.at[:, pl.ds(base, WINDOW), :], buf.at[a, p], sems.at[a, p]
            )
            copy.start()
            copies.append((a, p, copy))
    lane = lax.broadcasted_iota(jnp.int32, (OCC * PIECE, LANES), 1)
    for a, p, copy in copies:
        start = start_ref[p]
        offset = start - jnp.minimum(start // 16 * 16, WIDTH - WINDOW)
        copy.wait()
        for i in range(OCC):
            tail = buf[a, p, i, :, HEAD:].astype(jnp.float32)
            blank = jnp.zeros((WINDOW, HEAD + LANES - VIRTUALS), jnp.float32)
            last[i, :, : HEAD - LAST] = buf[a, p, i, :, LAST:HEAD].astype(jnp.float32)
            last[i, :, HEAD - LAST : HEAD - LAST + LANES] = jnp.concatenate([tail, blank], axis=1)
        mine = jnp.zeros((OCC * PIECE, LANES), jnp.float32)
        for m in range(NV):
            column = m * WIDTH + start
            tile = column // LANES
            shift = lax.rem(m * PIECE + LANES - lax.rem(column, LANES), LANES)
            for half in range(2):
                if m < NV - 1:
                    lanes = pl.ds(pl.multiple_of((tile + half) * LANES, LANES), LANES)
                    rows[...] = buf[a, p, :, :, lanes].astype(jnp.float32)
                else:
                    lanes = pl.ds(pl.multiple_of((tile + half) * LANES - LAST, LANES), LANES)
                    rows[...] = last[:, :, lanes]
                parts = [rows[i, pl.ds(offset, PIECE), :] for i in range(OCC)]
                turned = pltpu.roll(jnp.concatenate(parts, axis=0), shift, 1)
                first = lax.rem(column, LANES)
                inside = (lane >= m * PIECE) & (lane < (m + 1) * PIECE)
                here = lane - m * PIECE + first
                inside = inside & ((here < LANES) if half == 0 else (here >= LANES))
                mine = jnp.where(inside, turned, mine)
        turned = mine.T
        if a == 0:
            flip[...] = turned
            for i in range(OCC):
                cells = [flip[pl.ds(q, PIECE, 4), :][:, PIECE * i : PIECE * (i + 1)] for q in range(4)]
                block = jnp.concatenate(cells, axis=1).astype(jnp.bfloat16)
                own_ref[pl.ds((p * OCC + i) * PIECE, PIECE), :] = block
                for z in range(NZ):
                    line_ref[z, pl.ds((p * OCC + i) * PIECE, PIECE), :] = block
        else:
            own_ref[pl.ds(AMP_ROWS + p * PANEL, PANEL), :] = turned.astype(jnp.bfloat16)


def cut(panel_start, amps, lams):
    return pl.pallas_call(
        cut_kernel,
        out_shape=(
            jax.ShapeDtypeStruct((NZ, AMP_ROWS, LANES), jnp.bfloat16),
            jax.ShapeDtypeStruct((AMP_ROWS + LAM_ROWS, LANES), jnp.bfloat16),
        ),
        in_specs=[
            pl.BlockSpec(memory_space=pltpu.SMEM),
            pl.BlockSpec(memory_space=pltpu.HBM),
            pl.BlockSpec(memory_space=pltpu.HBM),
        ],
        out_specs=(pl.BlockSpec(memory_space=pltpu.VMEM),) * 2,
        scratch_shapes=[
            pltpu.VMEM((2, PANELS, OCC, WINDOW, VIRTUALS), jnp.bfloat16),
            pltpu.VMEM((OCC, WINDOW, LANES), jnp.float32),
            pltpu.VMEM((OCC, WINDOW, HEAD - LAST + 2 * LANES), jnp.float32),
            pltpu.VMEM((LANES, LANES), jnp.float32),
            pltpu.SemaphoreType.DMA((2, PANELS)),
        ],
        compiler_params=pltpu.CompilerParams(vmem_limit_bytes=56 * 2**20),
        name="cut_panels",
    )(panel_start, amps, lams)


def rows_kernel(near_ref, out_ref, wide):
    for p in range(PANELS):
        for k in range(NZ):
            part = near_ref[k, pl.ds(p * HALF, HALF), :]
            wide[pl.ds(k * HALF, HALF), :] = part.astype(jnp.float32)
        for r in range(PIECE):
            out_ref[p, :, pl.ds(r * LANES, LANES)] = wide[pl.ds(r, NZ * OCC, PIECE), :].astype(jnp.bfloat16)


def to_rows(near):
    vmem = pl.BlockSpec(memory_space=pltpu.VMEM)
    return pl.pallas_call(
        rows_kernel,
        out_shape=jax.ShapeDtypeStruct((PANELS, NZ * OCC, PIECE * LANES), jnp.bfloat16),
        in_specs=[vmem],
        out_specs=vmem,
        scratch_shapes=[pltpu.VMEM((NZ * HALF, LANES), jnp.float32)],
        compiler_params=pltpu.CompilerParams(vmem_limit_bytes=16 * 2**20),
        name="occupied_rows",
    )(near)


def plane_kernel(place_ref, *refs):
    ins, out_ref, pick, prod, wide, own = refs[:NXY], *refs[NXY:]
    xy = place_ref[0]
    lane = lax.broadcasted_iota(jnp.int32, (OCC * 4, LANES), 1) // PIECE
    for p in range(PANELS):
        for s in range(NXY):
            wide[...] = ins[s][pl.ds(p * HALF, HALF), :].astype(jnp.float32)
            amp = jnp.concatenate([wide[pl.ds(j * PIECE + 4 * xy, 4), :] for j in range(OCC)], axis=0)
            for d in range(4):
                turned = amp if d == 0 else pltpu.roll(amp, PIECE * d, 1)
                for i in range(OCC):
                    row = (i - d) % 4 * 64 + i * 16
                    pick[pl.ds(row, 16), pl.ds(s * LANES, LANES)] = jnp.where(lane == i, turned, 0.0).astype(jnp.bfloat16)
            row = pl.multiple_of(AMP_ROWS + p * PANEL + 16 * xy, 16)
            own[s, p] = ins[s][pl.ds(row, 16), :].astype(jnp.float32)
        lam = jnp.concatenate([ins[s][pl.ds(AMP_ROWS + p * PANEL, PANEL), :] for s in range(NXY)], axis=1)
        prod[...] = lax.dot_general(pick[...], lam, (((1,), (1,)), ((), ())), preferred_element_type=jnp.float32)
        for z in range(NZ):
            for beta in range(2):
                for j in range(OCC):
                    row = (z % 2 * 2 + beta) * 64 + j * 4 + z // 2
                    out_ref[z, pl.ds(p * 32 + beta * 16 + j * 4, OCC), :] = prod[pl.ds(row, OCC, 16), :]
    for z in range(NZ):
        for s in range(NXY):
            for p in range(PANELS):
                out_ref[z, pl.ds(PART_ROWS + s * 4 + p * 2, 2), :] = own[s, p, pl.ds(2 * z, 2), :]


def plane_share(place, parts):
    vmem = pl.BlockSpec(memory_space=pltpu.VMEM)
    return pl.pallas_call(
        plane_kernel,
        out_shape=jax.ShapeDtypeStruct((NZ, PART_ROWS + OWN_ROWS, LANES), jnp.float32),
        in_specs=[pl.BlockSpec(memory_space=pltpu.SMEM)] + [vmem] * NXY,
        out_specs=vmem,
        scratch_shapes=[
            pltpu.VMEM((2 * LANES, NXY * LANES), jnp.bfloat16),
            pltpu.VMEM((2 * LANES, LANES), jnp.float32),
            pltpu.VMEM((HALF, LANES), jnp.float32),
            pltpu.VMEM((NXY, PANELS, 16, LANES), jnp.float32),
        ],
        compiler_params=pltpu.CompilerParams(vmem_limit_bytes=16 * 2**20),
        name="plane_share",
    )(place, *parts)


def pack_kernel(in_ref, out_ref, rows):
    total = in_ref[0, pl.ds(0, PART_ROWS), :]
    for z in range(1, NZ):
        total = total + in_ref[z, pl.ds(0, PART_ROWS), :]
    for z in range(NZ):
        for s in range(NXY):
            rows[pl.ds((s * NZ + z) * 4, 4), :] = in_ref[z, pl.ds(PART_ROWS + s * 4, 4), :]
    out_ref[pl.ds(0, NZ * OWN_ROWS), :] = rows[...].astype(jnp.bfloat16)
    high = total.astype(jnp.bfloat16)
    out_ref[pl.ds(NZ * OWN_ROWS, PART_ROWS), :] = high
    out_ref[pl.ds(NZ * OWN_ROWS + PART_ROWS, PART_ROWS), :] = (total - high.astype(jnp.float32)).astype(jnp.bfloat16)


def pack(got):
    vmem = pl.BlockSpec(memory_space=pltpu.VMEM)
    return pl.pallas_call(
        pack_kernel,
        out_shape=jax.ShapeDtypeStruct((NZ * OWN_ROWS + 2 * PART_ROWS, LANES), jnp.bfloat16),
        in_specs=[vmem],
        out_specs=vmem,
        scratch_shapes=[pltpu.VMEM((NZ * OWN_ROWS, LANES), jnp.float32)],
        compiler_params=pltpu.CompilerParams(vmem_limit_bytes=8 * 2**20),
        name="pack_shares",
    )(got)


def lam_kernel(place_ref, own_ref, line_ref, part_ref, wide, rows):
    lane = lax.broadcasted_iota(jnp.int32, (NXY * NZ, LANES), 1) // PIECE
    count = NXY * OWN_ROWS
    wide[...] = own_ref[:, pl.ds(0, count), :].astype(jnp.float32)
    for p in range(PANELS):
        for g in range(2):
            parts = [wide[v, pl.ds(2 * p + g, NXY * NZ, 4), :] for v in range(NV)]
            for i in range(OCC):
                cell = jnp.zeros((NXY * NZ, LANES), jnp.float32)
                for v in range(NV):
                    turn = PIECE * ((v - i) % 4)
                    part = parts[v] if turn == 0 else pltpu.roll(parts[v], turn, 1)
                    cell = jnp.where(lane == v, part, cell)
                rows[pl.ds(i, NXY * NZ, OCC), :] = cell
            line_ref[p, :, pl.ds(g * LANES, LANES)] = rows[...].astype(jnp.bfloat16)
    total = jnp.zeros((PART_ROWS, LANES), jnp.float32)
    for v in range(NV):
        for n in range(2):
            total = total + own_ref[v, pl.ds(count + n * PART_ROWS, PART_ROWS), :].astype(jnp.float32)
    mine = pltpu.roll(-total, lax.rem(LANES - place_ref[1] * PIECE, LANES), 1)
    part_ref[...] = mine[:, :PIECE].astype(jnp.bfloat16)


def lam_matrix(place, own):
    vmem = pl.BlockSpec(memory_space=pltpu.VMEM)
    matrix = jax.ShapeDtypeStruct((PANELS, PAIRS * OCC, 2 * LANES), jnp.bfloat16)
    return pl.pallas_call(
        lam_kernel,
        out_shape=(matrix, jax.ShapeDtypeStruct((PART_ROWS, PIECE), jnp.bfloat16)),
        in_specs=[pl.BlockSpec(memory_space=pltpu.SMEM), vmem],
        out_specs=(vmem, vmem),
        scratch_shapes=[
            pltpu.VMEM((NV, NXY * OWN_ROWS, LANES), jnp.float32),
            pltpu.VMEM((PAIRS * OCC, LANES), jnp.float32),
        ],
        compiler_params=pltpu.CompilerParams(vmem_limit_bytes=16 * 2**20),
        name="lam_matrix",
    )(place, own)


CHUNK = 4096
SLOTS = 2


def vvvv_kernel(*refs):
    blocks, lam_ref, part_ref, out_ref, ovov_ref, wide, stage, late, sems = refs[:NXY], *refs[NXY:]
    part_copy = pltpu.make_async_copy(part_ref, ovov_ref, sems.at[SLOTS])
    part_copy.start()
    chunks = PANELS * PIECE * LANES // CHUNK

    def fetch(n, p):
        return pltpu.make_async_copy(blocks[3 + 2 * n].at[p], late.at[p, n], sems.at[SLOTS + 1 + 3 * p + n])

    for p in range(PANELS):
        for n in range(3):
            fetch(n, p).start()

    def store(n):
        slot = lax.rem(n, SLOTS)
        row = pl.multiple_of(n * 2 * CHUNK, 2 * CHUNK)
        return pltpu.make_async_copy(stage.at[slot], out_ref.at[pl.ds(row, 2 * CHUNK), :], sems.at[slot])

    def step(n, carry):
        p = n // (chunks // PANELS)
        lanes = pl.ds(pl.multiple_of(lax.rem(n, chunks // PANELS) * CHUNK, CHUNK), CHUNK)

        @pl.when(lax.rem(n, chunks // PANELS) == 0)
        def _():
            for m in range(3):
                fetch(m, p).wait()

        parts = [late[p, (s - 3) // 2, :, lanes] if s in (3, 5, 7) else blocks[s][p, :, lanes] for s in range(NXY)]
        amp = jnp.concatenate(parts, axis=0)
        prod = lax.dot_general(amp, lam_ref[p], (((0,), (0,)), ((), ())), preferred_element_type=jnp.float32)
        prod = prod * 0.5
        wide[pl.ds(0, CHUNK, 2), :] = prod[:, :LANES]
        wide[pl.ds(1, CHUNK, 2), :] = prod[:, LANES:]

        @pl.when(n >= SLOTS)
        def _():
            store(n - SLOTS).wait()

        stage[lax.rem(n, SLOTS)] = wide[...].astype(jnp.bfloat16)
        store(n).start()
        return carry

    lax.fori_loop(0, chunks, step, 0)
    for n in range(chunks - SLOTS, chunks):
        store(n).wait()
    part_copy.wait()


def vvvv_product(blocks, lam, part):
    vmem = pl.BlockSpec(memory_space=pltpu.VMEM)
    out, ovov = pl.pallas_call(
        vvvv_kernel,
        out_shape=(
            jax.ShapeDtypeStruct((PANELS * PANEL * PIECE * 2, LANES), jnp.bfloat16),
            jax.ShapeDtypeStruct(part.shape, part.dtype),
        ),
        in_specs=[pl.BlockSpec(memory_space=pl.ANY) if s in (3, 5, 7) else vmem for s in range(NXY)] + [vmem] * 2,
        out_specs=(pl.BlockSpec(memory_space=pltpu.HBM),) * 2,
        scratch_shapes=[
            pltpu.VMEM((2 * CHUNK, LANES), jnp.float32),
            pltpu.VMEM((SLOTS, 2 * CHUNK, LANES), jnp.bfloat16),
            pltpu.VMEM((PANELS, 3, NZ * OCC, PIECE * LANES), jnp.bfloat16),
            pltpu.SemaphoreType.DMA((SLOTS + 1 + 3 * PANELS,)),
        ],
        compiler_params=pltpu.CompilerParams(vmem_limit_bytes=32 * 2**20),
        name="vvvv_product",
    )(*blocks, lam, part)
    return out.reshape(PANELS, PANEL, PIECE, 2, LANES), ovov.reshape(PANELS, 2, OCC, OCC, PIECE)


def send(block, dy, dx):
    return lax.ppermute(block, "pair", pair_shift(dy, dx))


def after(value, *others):
    return lax.optimization_barrier((value,) + others)[0]


def shards(t2_amps, l2_amps, panel_start):
    amps = jnp.transpose(t2_amps[:, 0], (0, 2, 1))
    lams = jnp.transpose(l2_amps[:, 0], (0, 2, 1))
    place = jnp.stack([lax.axis_index("pair") // NZ, lax.axis_index("virt")]).astype(jnp.int32)
    parcel, own = cut(panel_start, amps, lams)
    near = lax.all_to_all(parcel, "pair", 0, 0, axis_index_groups=Z_GROUPS)

    there = send(own, 1, 0)
    plane = [own, there]
    for dx in X_SHIFTS:
        near_own = send(own, 0, dx)
        plane += [near_own, send(near_own, 1, 0) if dx == 2 else send(there, 0, dx)]
    near = after(near, *plane)

    held = to_rows(near)
    other = send(held, 1, 0)
    beside = {dx: send(held, 0, dx) for dx in X_SHIFTS}
    cross = {1: send(other, 0, 1), 3: send(other, 0, 3), 2: send(beside[2], 1, 0)}
    blocks = [held, other]
    for dx in X_SHIFTS:
        blocks += [beside[dx], cross[dx]]

    share = lax.all_to_all(plane_share(place, plane), "pair", 0, 0, axis_index_groups=Z_GROUPS)
    rows = after(pack(share), other)
    lam, part = lam_matrix(place, lax.all_gather(rows, "virt"))
    return vvvv_product(blocks, lam, part)


def solution(mesh):
    in_specs = (P(None, "pair", None, "virt"), P(None, "pair", None, "virt"), P())
    out_specs = (P(None, None, "virt", "pair", None), P(None, "pair", None, None, "virt"))
    return jax.shard_map(shards, mesh=mesh, in_specs=in_specs, out_specs=out_specs, check_vma=False)
```

```python
import functools

import jax
import jax.numpy as jnp
from jax import lax
from jax.experimental import pallas as pl
from jax.experimental.pallas import tpu as pltpu
from jax.sharding import PartitionSpec as P

NZ = 8
NX = 4
NY = 2
NXY = NX * NY
PAIRS = NZ * NXY
PANELS = 2
NV = 4
OCC = 4
PANEL = 128
PIECE = PANEL // NV
LANES = 128
VIRTUALS = 1600
WIDTH = VIRTUALS // NV
WINDOW = PIECE + 16
HEAD = VIRTUALS // LANES * LANES
LAST = (VIRTUALS - WIDTH) // LANES * LANES
AMP_ROWS = PANELS * OCC * PIECE
LAM_ROWS = PANELS * PANEL
Z_GROUPS = [[xy * NZ + z for z in range(NZ)] for xy in range(NXY)]
X_SHIFTS = (1, 3, 2)
HALF = AMP_ROWS // PANELS
PART_ROWS = 64
OWN_ROWS = NXY * PANELS * 2


def pair_shift(dy, dx):
    return [
        ((y * NX + x) * NZ + z, (((y + dy) % NY) * NX + (x + dx) % NX) * NZ + z)
        for y in range(NY)
        for x in range(NX)
        for z in range(NZ)
    ]


def cut_kernel(start_ref, amp_ref, lam_ref, line_ref, own_ref, buf, rows, last, flip, sems):
    copies = []
    for a, src in enumerate((amp_ref, lam_ref)):
        for p in range(PANELS):
            base = jnp.minimum(start_ref[p] // 16 * 16, WIDTH - WINDOW)
            base = pl.multiple_of(base, 16)
            copy = pltpu.make_async_copy(
                src.at[:, pl.ds(base, WINDOW), :], buf.at[a, p], sems.at[a, p]
            )
            copy.start()
            copies.append((a, p, copy))
    lane = lax.broadcasted_iota(jnp.int32, (OCC * PIECE, LANES), 1)
    for a, p, copy in copies:
        start = start_ref[p]
        offset = start - jnp.minimum(start // 16 * 16, WIDTH - WINDOW)
        copy.wait()
        for i in range(OCC):
            tail = buf[a, p, i, :, HEAD:].astype(jnp.float32)
            blank = jnp.zeros((WINDOW, HEAD + LANES - VIRTUALS), jnp.float32)
            last[i, :, : HEAD - LAST] = buf[a, p, i, :, LAST:HEAD].astype(jnp.float32)
            last[i, :, HEAD - LAST : HEAD - LAST + LANES] = jnp.concatenate([tail, blank], axis=1)
        mine = jnp.zeros((OCC * PIECE, LANES), jnp.float32)
        for m in range(NV):
            column = m * WIDTH + start
            tile = column // LANES
            shift = lax.rem(m * PIECE + LANES - lax.rem(column, LANES), LANES)
            for half in range(2):
                if m < NV - 1:
                    lanes = pl.ds(pl.multiple_of((tile + half) * LANES, LANES), LANES)
                    rows[...] = buf[a, p, :, :, lanes].astype(jnp.float32)
                else:
                    lanes = pl.ds(pl.multiple_of((tile + half) * LANES - LAST, LANES), LANES)
                    rows[...] = last[:, :, lanes]
                parts = [rows[i, pl.ds(offset, PIECE), :] for i in range(OCC)]
                turned = pltpu.roll(jnp.concatenate(parts, axis=0), shift, 1)
                first = lax.rem(column, LANES)
                inside = (lane >= m * PIECE) & (lane < (m + 1) * PIECE)
                here = lane - m * PIECE + first
                inside = inside & ((here < LANES) if half == 0 else (here >= LANES))
                mine = jnp.where(inside, turned, mine)
        turned = mine.T
        if a == 0:
            flip[...] = turned
            for i in range(OCC):
                cells = [flip[pl.ds(q, PIECE, 4), :][:, PIECE * i : PIECE * (i + 1)] for q in range(4)]
                block = jnp.concatenate(cells, axis=1).astype(jnp.bfloat16)
                own_ref[pl.ds((p * OCC + i) * PIECE, PIECE), :] = block
                for z in range(NZ):
                    line_ref[z, pl.ds((p * OCC + i) * PIECE, PIECE), :] = block
        else:
            own_ref[pl.ds(AMP_ROWS + p * PANEL, PANEL), :] = turned.astype(jnp.bfloat16)


def cut(panel_start, amps, lams):
    return pl.pallas_call(
        cut_kernel,
        out_shape=(
            jax.ShapeDtypeStruct((NZ, AMP_ROWS, LANES), jnp.bfloat16),
            jax.ShapeDtypeStruct((AMP_ROWS + LAM_ROWS, LANES), jnp.bfloat16),
        ),
        in_specs=[
            pl.BlockSpec(memory_space=pltpu.SMEM),
            pl.BlockSpec(memory_space=pltpu.HBM),
            pl.BlockSpec(memory_space=pltpu.HBM),
        ],
        out_specs=(pl.BlockSpec(memory_space=pltpu.VMEM),) * 2,
        scratch_shapes=[
            pltpu.VMEM((2, PANELS, OCC, WINDOW, VIRTUALS), jnp.bfloat16),
            pltpu.VMEM((OCC, WINDOW, LANES), jnp.float32),
            pltpu.VMEM((OCC, WINDOW, HEAD - LAST + 2 * LANES), jnp.float32),
            pltpu.VMEM((LANES, LANES), jnp.float32),
            pltpu.SemaphoreType.DMA((2, PANELS)),
        ],
        compiler_params=pltpu.CompilerParams(vmem_limit_bytes=56 * 2**20),
        name="cut_panels",
    )(panel_start, amps, lams)


def rows_kernel(near_ref, out_ref, wide):
    for p in range(PANELS):
        for k in range(NZ):
            part = near_ref[k, pl.ds(p * HALF, HALF), :]
            wide[pl.ds(k * HALF, HALF), :] = part.astype(jnp.float32)
        for r in range(PIECE):
            out_ref[p, :, pl.ds(r * LANES, LANES)] = wide[pl.ds(r, NZ * OCC, PIECE), :].astype(jnp.bfloat16)


def to_rows(near):
    vmem = pl.BlockSpec(memory_space=pltpu.VMEM)
    return pl.pallas_call(
        rows_kernel,
        out_shape=jax.ShapeDtypeStruct((PANELS, NZ * OCC, PIECE * LANES), jnp.bfloat16),
        in_specs=[vmem],
        out_specs=vmem,
        scratch_shapes=[pltpu.VMEM((NZ * HALF, LANES), jnp.float32)],
        compiler_params=pltpu.CompilerParams(vmem_limit_bytes=16 * 2**20),
        name="occupied_rows",
    )(near)


def plane_kernel(place_ref, *refs):
    ins, out_ref, pick, prod, wide, own = refs[:NXY], *refs[NXY:]
    xy = place_ref[0]
    lane = lax.broadcasted_iota(jnp.int32, (OCC * 4, LANES), 1) // PIECE
    for p in range(PANELS):
        for s in range(NXY):
            wide[...] = ins[s][pl.ds(p * HALF, HALF), :].astype(jnp.float32)
            amp = jnp.concatenate([wide[pl.ds(j * PIECE + 4 * xy, 4), :] for j in range(OCC)], axis=0)
            for d in range(4):
                turned = amp if d == 0 else pltpu.roll(amp, PIECE * d, 1)
                for i in range(OCC):
                    row = (i - d) % 4 * 64 + i * 16
                    pick[pl.ds(row, 16), pl.ds(s * LANES, LANES)] = jnp.where(lane == i, turned, 0.0).astype(jnp.bfloat16)
            row = pl.multiple_of(AMP_ROWS + p * PANEL + 16 * xy, 16)
            own[s, p] = ins[s][pl.ds(row, 16), :].astype(jnp.float32)
        lam = jnp.concatenate([ins[s][pl.ds(AMP_ROWS + p * PANEL, PANEL), :] for s in range(NXY)], axis=1)
        prod[...] = lax.dot_general(pick[...], lam, (((1,), (1,)), ((), ())), preferred_element_type=jnp.float32)
        for z in range(NZ):
            for beta in range(2):
                for j in range(OCC):
                    row = (z % 2 * 2 + beta) * 64 + j * 4 + z // 2
                    out_ref[z, pl.ds(p * 32 + beta * 16 + j * 4, OCC), :] = prod[pl.ds(row, OCC, 16), :]
    for z in range(NZ):
        for s in range(NXY):
            for p in range(PANELS):
                out_ref[z, pl.ds(PART_ROWS + s * 4 + p * 2, 2), :] = own[s, p, pl.ds(2 * z, 2), :]


def plane_share(place, parts):
    vmem = pl.BlockSpec(memory_space=pltpu.VMEM)
    return pl.pallas_call(
        plane_kernel,
        out_shape=jax.ShapeDtypeStruct((NZ, PART_ROWS + OWN_ROWS, LANES), jnp.float32),
        in_specs=[pl.BlockSpec(memory_space=pltpu.SMEM)] + [vmem] * NXY,
        out_specs=vmem,
        scratch_shapes=[
            pltpu.VMEM((2 * LANES, NXY * LANES), jnp.bfloat16),
            pltpu.VMEM((2 * LANES, LANES), jnp.float32),
            pltpu.VMEM((HALF, LANES), jnp.float32),
            pltpu.VMEM((NXY, PANELS, 16, LANES), jnp.float32),
        ],
        compiler_params=pltpu.CompilerParams(vmem_limit_bytes=16 * 2**20),
        name="plane_share",
    )(place, *parts)


def pack_kernel(in_ref, out_ref, rows):
    total = in_ref[0, pl.ds(0, PART_ROWS), :]
    for z in range(1, NZ):
        total = total + in_ref[z, pl.ds(0, PART_ROWS), :]
    for z in range(NZ):
        for s in range(NXY):
            rows[pl.ds((s * NZ + z) * 4, 4), :] = in_ref[z, pl.ds(PART_ROWS + s * 4, 4), :]
    out_ref[pl.ds(0, NZ * OWN_ROWS), :] = rows[...].astype(jnp.bfloat16)
    high = total.astype(jnp.bfloat16)
    out_ref[pl.ds(NZ * OWN_ROWS, PART_ROWS), :] = high
    out_ref[pl.ds(NZ * OWN_ROWS + PART_ROWS, PART_ROWS), :] = (total - high.astype(jnp.float32)).astype(jnp.bfloat16)


def pack(got):
    vmem = pl.BlockSpec(memory_space=pltpu.VMEM)
    return pl.pallas_call(
        pack_kernel,
        out_shape=jax.ShapeDtypeStruct((NZ * OWN_ROWS + 2 * PART_ROWS, LANES), jnp.bfloat16),
        in_specs=[vmem],
        out_specs=vmem,
        scratch_shapes=[pltpu.VMEM((NZ * OWN_ROWS, LANES), jnp.float32)],
        compiler_params=pltpu.CompilerParams(vmem_limit_bytes=8 * 2**20),
        name="pack_shares",
    )(got)


def lam_kernel(place_ref, own_ref, line_ref, part_ref, wide, rows):
    lane = lax.broadcasted_iota(jnp.int32, (NXY * NZ, LANES), 1) // PIECE
    count = NXY * OWN_ROWS
    wide[...] = own_ref[:, pl.ds(0, count), :].astype(jnp.float32)
    for p in range(PANELS):
        for g in range(2):
            parts = [wide[v, pl.ds(2 * p + g, NXY * NZ, 4), :] for v in range(NV)]
            for i in range(OCC):
                cell = jnp.zeros((NXY * NZ, LANES), jnp.float32)
                for v in range(NV):
                    turn = PIECE * ((v - i) % 4)
                    part = parts[v] if turn == 0 else pltpu.roll(parts[v], turn, 1)
                    cell = jnp.where(lane == v, part, cell)
                rows[pl.ds(i, NXY * NZ, OCC), :] = cell
            line_ref[p, :, pl.ds(g * LANES, LANES)] = rows[...].astype(jnp.bfloat16)
    total = jnp.zeros((PART_ROWS, LANES), jnp.float32)
    for v in range(NV):
        for n in range(2):
            total = total + own_ref[v, pl.ds(count + n * PART_ROWS, PART_ROWS), :].astype(jnp.float32)
    mine = pltpu.roll(-total, lax.rem(LANES - place_ref[1] * PIECE, LANES), 1)
    part_ref[...] = mine[:, :PIECE].astype(jnp.bfloat16)


def lam_matrix(place, own):
    vmem = pl.BlockSpec(memory_space=pltpu.VMEM)
    matrix = jax.ShapeDtypeStruct((PANELS, PAIRS * OCC, 2 * LANES), jnp.bfloat16)
    return pl.pallas_call(
        lam_kernel,
        out_shape=(matrix, jax.ShapeDtypeStruct((PART_ROWS, PIECE), jnp.bfloat16)),
        in_specs=[pl.BlockSpec(memory_space=pltpu.SMEM), vmem],
        out_specs=(vmem, vmem),
        scratch_shapes=[
            pltpu.VMEM((NV, NXY * OWN_ROWS, LANES), jnp.float32),
            pltpu.VMEM((PAIRS * OCC, LANES), jnp.float32),
        ],
        compiler_params=pltpu.CompilerParams(vmem_limit_bytes=16 * 2**20),
        name="lam_matrix",
    )(place, own)


CHUNK = 4096
SLOTS = 2


def vvvv_kernel(*refs):
    blocks, lam_ref, part_ref, out_ref, ovov_ref, wide, stage, late, sems, halves = refs[:NXY], *refs[NXY:]
    part_copy = pltpu.make_async_copy(part_ref, ovov_ref, sems.at[SLOTS])
    part_copy.start()
    chunks = PANELS * PIECE * LANES // CHUNK

    def fetch(n, p):
        return pltpu.make_async_copy(blocks[3 + 2 * n].at[p], late.at[p, n], sems.at[SLOTS + 1 + 3 * p + n])

    for p in range(PANELS):
        for n in range(3):
            fetch(n, p).start()

    def store(n, half):
        slot = lax.rem(n, SLOTS)
        row = pl.multiple_of((2 * n + half) * CHUNK, CHUNK)
        return pltpu.make_async_copy(
            stage.at[slot, pl.ds(half * CHUNK, CHUNK), :], out_ref.at[pl.ds(row, CHUNK), :], halves.at[slot, half]
        )

    def step(n, carry):
        p = n // (chunks // PANELS)
        lanes = pl.ds(pl.multiple_of(lax.rem(n, chunks // PANELS) * CHUNK, CHUNK), CHUNK)

        @pl.when(lax.rem(n, chunks // PANELS) == 0)
        def _():
            for m in range(3):
                fetch(m, p).wait()

        parts = [late[p, (s - 3) // 2, :, lanes] if s in (3, 5, 7) else blocks[s][p, :, lanes] for s in range(NXY)]
        amp = jnp.concatenate(parts, axis=0)
        prod = lax.dot_general(amp, lam_ref[p], (((0,), (0,)), ((), ())), preferred_element_type=jnp.float32)
        prod = prod * 0.5
        wide[pl.ds(0, CHUNK, 2), :] = prod[:, :LANES]
        wide[pl.ds(1, CHUNK, 2), :] = prod[:, LANES:]

        @pl.when(n >= SLOTS)
        def _():
            store(n - SLOTS, 0).wait()
            store(n - SLOTS, 1).wait()

        for half in range(2):
            rows = pl.ds(half * CHUNK, CHUNK)
            stage[lax.rem(n, SLOTS), rows, :] = wide[rows, :].astype(jnp.bfloat16)
            store(n, half).start()
        return carry

    lax.fori_loop(0, chunks, step, 0)
    for n in range(chunks - SLOTS, chunks):
        store(n, 0).wait()
        store(n, 1).wait()
    part_copy.wait()


def vvvv_product(blocks, lam, part):
    vmem = pl.BlockSpec(memory_space=pltpu.VMEM)
    out, ovov = pl.pallas_call(
        vvvv_kernel,
        out_shape=(
            jax.ShapeDtypeStruct((PANELS * PANEL * PIECE * 2, LANES), jnp.bfloat16),
            jax.ShapeDtypeStruct(part.shape, part.dtype),
        ),
        in_specs=[pl.BlockSpec(memory_space=pl.ANY) if s in (3, 5, 7) else vmem for s in range(NXY)] + [vmem] * 2,
        out_specs=(pl.BlockSpec(memory_space=pltpu.HBM),) * 2,
        scratch_shapes=[
            pltpu.VMEM((2 * CHUNK, LANES), jnp.float32),
            pltpu.VMEM((SLOTS, 2 * CHUNK, LANES), jnp.bfloat16),
            pltpu.VMEM((PANELS, 3, NZ * OCC, PIECE * LANES), jnp.bfloat16),
            pltpu.SemaphoreType.DMA((SLOTS + 1 + 3 * PANELS,)),
            pltpu.SemaphoreType.DMA((SLOTS, 2)),
        ],
        compiler_params=pltpu.CompilerParams(vmem_limit_bytes=32 * 2**20),
        name="vvvv_product",
    )(*blocks, lam, part)
    return out.reshape(PANELS, PANEL, PIECE, 2, LANES), ovov.reshape(PANELS, 2, OCC, OCC, PIECE)


def send(block, dy, dx):
    return lax.ppermute(block, "pair", pair_shift(dy, dx))


def after(value, *others):
    return lax.optimization_barrier((value,) + others)[0]


def shards(t2_amps, l2_amps, panel_start):
    amps = jnp.transpose(t2_amps[:, 0], (0, 2, 1))
    lams = jnp.transpose(l2_amps[:, 0], (0, 2, 1))
    place = jnp.stack([lax.axis_index("pair") // NZ, lax.axis_index("virt")]).astype(jnp.int32)
    parcel, own = cut(panel_start, amps, lams)
    near = lax.all_to_all(parcel, "pair", 0, 0, axis_index_groups=Z_GROUPS)

    there = send(own, 1, 0)
    plane = [own, there]
    for dx in X_SHIFTS:
        near_own = send(own, 0, dx)
        plane += [near_own, send(near_own, 1, 0) if dx == 2 else send(there, 0, dx)]
    near = after(near, *plane)

    held = to_rows(near)
    other = send(held, 1, 0)
    beside = {dx: send(held, 0, dx) for dx in X_SHIFTS}
    cross = {1: send(other, 0, 1), 3: send(other, 0, 3), 2: send(beside[2], 1, 0)}
    blocks = [held, other]
    for dx in X_SHIFTS:
        blocks += [beside[dx], cross[dx]]

    share = lax.all_to_all(plane_share(place, plane), "pair", 0, 0, axis_index_groups=Z_GROUPS)
    rows = after(pack(share), other)
    lam, part = lam_matrix(place, lax.all_gather(rows, "virt"))
    return vvvv_product(blocks, lam, part)


def solution(mesh):
    in_specs = (P(None, "pair", None, "virt"), P(None, "pair", None, "virt"), P())
    out_specs = (P(None, None, "virt", "pair", None), P(None, "pair", None, None, "virt"))
    return jax.shard_map(shards, mesh=mesh, in_specs=in_specs, out_specs=out_specs, check_vma=False)
```
